256 devices in a mesh: tile: 64 (over y, z, core), pair: 4 (over x).
Axes of the slice: x: 4, y: 4, z: 8, core: 2. Of those that a mesh axis runs over, the one named last changes fastest.
Arguments:
- fixed_image: bfloat16 [4, 32768, 512], P('pair', 'tile'), may hold values from -6 to 6
- moving_patches: bfloat16 [4, 2048, 160, 160], P('pair', 'tile'), may hold values from -6 to 6
- owners: int32 [4, 2048], P('pair', 'tile'), may hold values from 0 to 63, as said below
- offsets: int32 [4, 2048, 2], P('pair', 'tile'), may hold values from 0 to 352
- mobility: float32 [4, 1024, 512], P('pair', 'tile'), may hold values from 0.3 to 1
- prior_flow: float32 [4, 2, 1024, 512], P('pair', None, 'tile'), may hold values from -4 to 4
Outputs:
- patch_flow: float32 [4, 2, 2048], P('pair', None, 'tile')
- displacement: float32 [4, 2, 1024, 512], P('pair', None, 'tile')
The draws below stay inside these ranges and needn't reach their ends.
Inputs may be any that keep to these rules, and one draw needn't show every extreme that they name: `owners`: within one section pair, each owner is named by at most 2 patches of any one device's 32 patches and by at most 64 patches in all; both bounds are reached in every draw.
All inputs are finite; a program needn't handle non-finite values.
Results may differ from the reference program's by a relative error of at most 0.015.
Values may be sent and summed in bfloat16 or wider, within the bound.
A program may use at most 128 MiB of HBM per device.

```python
import math
import jax
import jax.numpy as jnp
from jax import lax

W = 160
TILE = 512
PATCH_DEV = 32
NODE_X = 512
STEPS = 32
PAIRS = 4
PATCHES = 2048
TILES_Y = 32768
NODES_Y = 1024
STRIDE = 256


def draw_owners(key, part):
    key = jax.random.fold_in(key, 7)
    tile_count = PATCHES // PATCH_DEV

    def one_pair(pair_key):
        perm_key, shift_key, order_key = jax.random.split(pair_key, 3)
        ranking = jax.random.permutation(perm_key, tile_count).astype(jnp.int32)
        rotation = jax.random.randint(shift_key, (), 0, tile_count, dtype=jnp.int32)
        sources = jnp.arange(tile_count, dtype=jnp.int32)[:, None]
        within = jnp.arange(PATCH_DEV, dtype=jnp.int32)[None, :]
        couple = (sources - rotation) % tile_count + within // 2 * tile_count
        entry = 2 * couple + within % 2
        half_total = tile_count * PATCH_DEV // 2
        position = jnp.where(entry < half_total, entry // (2 * PATCH_DEV), tile_count // 4 + (entry - half_total) // PATCH_DEV)
        position = jnp.clip(position, 0, tile_count - 1)
        assigned = ranking[position]
        scores = jax.random.randint(order_key, (tile_count, PATCH_DEV), 0, 1 << 20, dtype=jnp.int32) * PATCH_DEV + within
        ordering = jnp.argsort(scores, axis=1, stable=True)
        return jnp.take_along_axis(assigned, ordering, axis=1).reshape(tile_count * PATCH_DEV).astype(jnp.int32)
    return jax.vmap(one_pair)(jax.random.split(key, PAIRS))


def plant(result, key, smallest, largest):
    longest = result.shape.index(max(result.shape))
    spots = []
    for shift in (0, 1):
        where = [jax.random.randint(jax.random.fold_in(key, axis), (), 0, length) for axis, length in enumerate(result.shape)]
        where[longest] = (where[longest] + shift) % result.shape[longest]
        spots.append(tuple(where))
    return result.at[spots[0]].set(smallest).at[spots[1]].set(largest)


def level_of(stream_key, shape, cuts, least, high):
    loudness, own = 1.0, jax.random.fold_in(stream_key, 6)
    for dim, blocks in cuts:
        steps = jnp.exp(jax.random.uniform(jax.random.fold_in(own, dim), (blocks,), jnp.float32, least / len(cuts), high / len(cuts)))
        loudness = loudness * jnp.repeat(steps, shape[dim] // blocks).reshape([-1 if axis == dim else 1 for axis in range(len(shape))])
    return loudness


def noise(own_key, extent, scale, bound, cuts=(), kind=jnp.bfloat16):
    factor_of = level_of(own_key, extent, cuts, -0.22, 0.18) if cuts else 1.0
    entries = jax.random.normal(own_key, extent, jnp.float32) * scale * factor_of
    return jnp.minimum(jnp.maximum(entries, -bound), bound).astype(kind)


def setup_inputs(seed: int = 0) -> dict:
    splits = jax.random.split(jax.random.key(seed), 7)
    fixed_image = noise(splits[0], (PAIRS, TILES_Y, TILE), 1.0, 6.0, ((0, 4), (1, 64)))
    moving_patches = noise(splits[1], (PAIRS, PATCHES, W, W), 1.0, 6.0, ((0, 4), (1, 64)))
    owners = draw_owners(jax.random.fold_in(splits[6], 71), 0)
    offsets = plant(jax.random.randint(splits[3], (PAIRS, PATCHES, 2), 0, TILE - W + 1), jax.random.fold_in(splits[3], 1), 0, TILE - W).astype(jnp.int32)
    mobility = jnp.clip(jnp.exp(math.log(1.0) - 1.2039728 * jax.random.uniform(splits[4], (PAIRS, NODES_Y, NODE_X), jnp.float32) ** level_of(splits[4], (PAIRS, NODES_Y, NODE_X), ((0, 4), (1, 64)), -0.2, 0.2)), 0.3, 1.0)
    prior_flow = noise(splits[5], (PAIRS, 2, NODES_Y, NODE_X), 1.0, 4.0, ((0, 4), (2, 64)), jnp.float32)
    return dict(fixed_image=fixed_image, moving_patches=moving_patches, owners=owners, offsets=offsets, mobility=mobility, prior_flow=prior_flow)


EPS = 1e-06

def make_tables():
    numbers = jnp.arange(W, dtype=jnp.int32)
    phase = (numbers[:, None] * numbers[None, :] % W).astype(jnp.float32) * (2.0 * math.pi / W)
    scale = 1.0 / math.sqrt(W)
    return ((jnp.cos(phase) * scale).astype(jnp.bfloat16), (jnp.sin(phase) * scale).astype(jnp.bfloat16))

def left_mul(table, batch):
    return jnp.einsum('ab,nbc->nac', table.astype(jnp.float32), batch.astype(jnp.float32), precision=lax.Precision.HIGHEST)

def right_mul(batch, table):
    return jnp.einsum('nab,bc->nac', batch.astype(jnp.float32), table.astype(jnp.float32), precision=lax.Precision.HIGHEST)

def spectrum(batch, cos_table, sin_table):
    a_part = left_mul(cos_table, batch).astype(jnp.bfloat16)
    b_part = left_mul(sin_table, batch).astype(jnp.bfloat16)
    real_part = (right_mul(a_part, cos_table) - right_mul(b_part, sin_table)).astype(jnp.bfloat16)
    imag_part = (-(right_mul(a_part, sin_table) + right_mul(b_part, cos_table))).astype(jnp.bfloat16)
    return (real_part, imag_part)

def block_flows(fixed_batch, moving_batch, cos_table, sin_table):
    fixed_re, fixed_im = spectrum(fixed_batch, cos_table, sin_table)
    moving_re, moving_im = spectrum(moving_batch, cos_table, sin_table)
    fr32 = fixed_re.astype(jnp.float32)
    fi32 = fixed_im.astype(jnp.float32)
    mr32 = moving_re.astype(jnp.float32)
    mi32 = moving_im.astype(jnp.float32)
    cross_re = (fr32 * mr32 + fi32 * mi32).astype(jnp.bfloat16)
    cross_im = (fi32 * mr32 - fr32 * mi32).astype(jnp.bfloat16)
    back_re = (left_mul(cos_table, cross_re) - left_mul(sin_table, cross_im)).astype(jnp.bfloat16)
    back_im = (left_mul(cos_table, cross_im) + left_mul(sin_table, cross_re)).astype(jnp.bfloat16)
    correlation = right_mul(back_re, cos_table) - right_mul(back_im, sin_table)
    energy = correlation * correlation
    total_energy = lax.optimization_barrier(jnp.sum(energy, axis=(1, 2))) + EPS
    numbers = jnp.arange(W, dtype=jnp.int32)
    signed_shift = jnp.where(numbers < W // 2, numbers, numbers - W).astype(jnp.float32)
    flow_rows = lax.optimization_barrier(jnp.sum(energy * signed_shift[None, :, None], axis=(1, 2))) / total_energy
    flow_cols = lax.optimization_barrier(jnp.sum(energy * signed_shift[None, None, :], axis=(1, 2))) / total_energy
    return jnp.stack([flow_rows, flow_cols], axis=1)

def reference(fixed_image, moving_patches, owners, offsets, mobility, prior_flow):
    cos_table, sin_table = make_tables()
    total = PAIRS * PATCHES
    block = math.gcd(total, 64)
    flat_moving = moving_patches.reshape(total // block, block, W, W)
    pair_index = (jnp.arange(total, dtype=jnp.int32) // PATCHES).astype(jnp.int32)
    row_start = (owners.reshape(total).astype(jnp.int32) * TILE + offsets[:, :, 0].reshape(total).astype(jnp.int32)).astype(jnp.int32)
    col_start = offsets[:, :, 1].reshape(total).astype(jnp.int32)

    def cut_one(which_pair, first_row, first_col):
        window = lax.dynamic_slice(fixed_image, (which_pair.astype(jnp.int32), first_row.astype(jnp.int32), first_col.astype(jnp.int32)), (1, W, W))
        return window[0]

    def one_block(pieces):
        pair_part, row_part, col_part, moving_part = pieces
        windows = jax.vmap(cut_one)(pair_part, row_part, col_part)
        return block_flows(windows, moving_part, cos_table, sin_table)
    flows = lax.map(one_block, (pair_index.reshape(-1, block), row_start.reshape(-1, block), col_start.reshape(-1, block), flat_moving))
    patch_flow = flows.reshape(PAIRS, PATCHES, 2).transpose(0, 2, 1)
    extra = jnp.zeros((PAIRS, 2, PATCHES, STRIDE), jnp.float32).at[:, :, :, STRIDE // 2].set(patch_flow)
    target = prior_flow + extra.reshape(PAIRS, 2, NODES_Y, NODE_X)
    weights = mobility[:, None]

    def relax(counter, carried):
        shifted, velocity = carried
        padded = jnp.pad(shifted, ((1, 1), (0, 0), (1, 1), (1, 1)), mode='edge')
        upper_rows = padded[1:-1, :, :-2, 1:-1]
        lower_rows = padded[1:-1, :, 2:, 1:-1]
        leftward = padded[1:-1, :, 1:-1, :-2]
        rightward = padded[1:-1, :, 1:-1, 2:]
        before = padded[:-2, :, 1:-1, 1:-1]
        following = padded[2:, :, 1:-1, 1:-1]
        laplace = upper_rows - shifted + (lower_rows - shifted) + (leftward - shifted) + (rightward - shifted)
        coupling = before - shifted + (following - shifted)
        forces = 0.35 * laplace + 0.2 * coupling + 0.3 * (target - shifted)
        velocity = 0.8 * velocity + weights * forces
        return (shifted + velocity, velocity)
    settled, last_velocity = lax.fori_loop(0, STEPS, relax, (prior_flow, jnp.zeros_like(prior_flow)))
    return (patch_flow, settled)
```

```python
import functools
import math

import jax
import jax.numpy as jnp
import ml_dtypes
import numpy as np
from jax import lax
from jax.experimental import pallas as pl
from jax.experimental.pallas import tpu as pltpu
from jax.sharding import PartitionSpec as P

MESH = pl.DeviceIdType.MESH
NY, NZ, NC, NP = 4, 8, 2, 4
TILES = NY * NZ * NC
W = 160
TILE = 512
PATCH_DEV = 32
STEPS = 32
EPS = 1e-06
ROWS = 16
COLS = 512
TILES_X = COLS // 128
HALO = 32
PAD = 8
SPAN = ROWS + 2 * HALO
HIGH = SPAN + 2 * PAD
HALF = W // 2 + 1
BLK = 88
FREQ = 2 * BLK
WIN_ROWS = 176
WIN_COLS = 384
MAX_SHIFT = 224
GROUP = 4
DEPTH = 2


def device_at(y, z, c):
    return {"tile": (y * NZ + z) * NC + c}


def my_place():
    t = lax.axis_index("tile")
    return t, t // (NZ * NC), (t // NC) % NZ, t % NC


def halo_targets(t, p):
    for dp in range(NP):
        for d in range(-2, 3):
            if dp or d:
                there = {"tile": (t + d + TILES) % TILES, "pair": (p + dp) % NP}
                yield dp, d, there


def remote(src, dst, send, recv, device):
    return pltpu.make_async_remote_copy(
        src_ref=src, dst_ref=dst, send_sem=send, recv_sem=recv, device_id=device, device_id_type=MESH
    )


def greet(devices):
    barrier = pltpu.get_barrier_semaphore()
    for device in devices:
        pl.semaphore_signal(barrier, inc=1, device_id=device, device_id_type=MESH)
    pl.semaphore_wait(barrier, len(devices))


def relax_block(target, u_in, u_out, vel, mob, mask_up, mask_dn, rows, tiles):
    here = pl.ds(rows, 8)
    up, dn = mask_up[here, :], mask_dn[here, :]
    lane = lax.broadcasted_iota(jnp.int32, (8, 128), 1)
    for comp in range(2):
        u = [[u_in[s, comp, n, here, :] for n in range(tiles)] for s in range(NP)]
        steps = [[u[s + 1][n] - u[s][n] for n in range(tiles)] for s in range(NP - 1)]
        for s in range(NP):
            turned = [pltpu.roll(u[s][n], 1, axis=1) for n in range(tiles)]
            left = []
            for n in range(tiles):
                if tiles > 1:
                    other = turned[n - 1] if n else u[s][0]
                    left.append(u[s][n] - jnp.where(lane == 0, other, turned[n]))
                else:
                    left.append(u[s][n] - turned[n])
            turned = [pltpu.roll(left[n], 127, axis=1) for n in range(tiles)]
            for n in range(tiles):
                right = turned[n]
                if tiles > 1:
                    right = jnp.where(lane == 127, turned[n + 1] if n + 1 < tiles else 0.0, right)
                above = u_in[s, comp, n, pl.ds(rows - 1, 8), :]
                below = u_in[s, comp, n, pl.ds(rows + 1, 8), :]
                lap = (below - u[s][n]) * dn - (u[s][n] - above) * up + (right - left[n])
                if s == 0:
                    inter = steps[0][n]
                elif s == NP - 1:
                    inter = -steps[s - 1][n]
                else:
                    inter = steps[s][n] - steps[s - 1][n]
                force = 0.35 * lap + 0.2 * inter + 0.3 * (target[s, comp, n, here, :] - u[s][n])
                speed = 0.8 * vel[s, comp, n, here, :] + mob(s, n, here) * force
                vel[s, comp, n, here, :] = speed
                u_out[s, comp, n, here, :] = u[s][n] + speed


def row_masks(t):
    row = t * ROWS - HALO - PAD + lax.broadcasted_iota(jnp.int32, (HIGH, 128), 0)
    return (row != 0).astype(jnp.float32), (row != TILES * ROWS - 1).astype(jnp.float32)


def gather_kernel(
    img, pat, meta, prior, mob, gi, gpl, gpr, gmeta, u_own, mob_band,
    pv, pr, own, net, uu, vel, mask_up, mask_dn,
    lsem, ysend, yrecv, zsend, zrecv, dsend, drecv, msend, mrecv, hsend, hrecv,
):
    t, y, z, c = my_place()
    p = lax.axis_index("pair")
    right_y, left_y = device_at((y + 1) % NY, z, c), device_at((y + NY - 1) % NY, z, c)
    right_z, left_z = device_at(y, (z + 1) % NZ, c), device_at(y, (z + NZ - 1) % NZ, c)
    across_y = device_at((y + 2) % NY, z, c)
    sibling = device_at(y, z, 1 - c)
    stage = pltpu.make_async_copy(pat, pv, lsem.at[0])
    stage.start()
    mine = z * NC + c
    keep = pltpu.make_async_copy(img, gi.at[mine], lsem.at[1])
    keep.start()
    halo = list(halo_targets(t, p))
    greet([right_y, left_y, across_y, right_z, left_z, sibling] + [device for _, _, device in halo])

    lo, hi = pl.ds(0, 16), pl.ds(16, 16)
    glo, ghi = pl.ds(0, 4), pl.ds(4, 4)
    left_part = pl.ds(0, 128)
    sent = []
    yr, yl = [], []

    def start(copy, into=None):
        copy.start()
        sent.append(copy)
        if into is not None:
            into.append(copy)
        return copy

    def y_left(which, first, side, device, slot):
        return remote(
            pat.at[which, :, left_part], gpl.at[first, which], ysend.at[side, slot], yrecv.at[side, slot], device
        )

    start(y_left(hi, y, 0, right_y, 0), yr)
    start(y_left(lo, y, 1, left_y, 0), yl)

    for n in range(TILES_X):
        columns = pl.ds(128 * n, 128)
        own[0:2, n] = prior[:, :, columns]
        own[2, n] = mob[:, columns]
    meshes = []
    for n, (dp, d, device) in enumerate(halo):
        rows = pl.ds(PAD + ROWS * (2 - d), ROWS)
        copy = remote(own, net.at[p, :, :, rows, :], hsend.at[n], hrecv.at[n], device)
        start(copy, meshes)

    half = TILE // 2
    zr, zl, dd = [], [], []
    for q in range(2):
        rs = pl.ds(q * half, half)
        start(remote(img.at[rs], gi.at[mine, rs], zsend.at[0, q], zrecv.at[0, q], right_z), zr)
        rs = pl.ds((1 - q) * half, half)
        start(remote(img.at[rs], gi.at[mine, rs], zsend.at[1, q], zrecv.at[1, q], left_z), zl)
    start(y_left(lo, y, 0, right_y, 1), yr)
    start(y_left(hi, y, 1, left_y, 1), yl)
    metas = []
    for n, device in enumerate((right_y, left_y, across_y)):
        start(remote(meta, gmeta.at[y], msend.at[n], mrecv.at[n], device), metas)
    start(remote(img, gi.at[mine], dsend.at[0], drecv.at[0], sibling), dd)

    stage.wait()
    for g in range(PATCH_DEV // 4):
        pr[g] = jnp.concatenate([pv[4 * g + q, :, 128:W] for q in range(4)], axis=1)
    pairs = []
    pairs.append(start(remote(pr.at[ghi], gpr.at[y, ghi], ysend.at[0, 3], yrecv.at[0, 3], right_y)))
    pairs.append(start(remote(pr.at[glo], gpr.at[y, glo], ysend.at[1, 3], yrecv.at[1, 3], left_y)))
    pairs.append(start(remote(pr.at[glo], gpr.at[y, glo], ysend.at[0, 4], yrecv.at[0, 4], right_y)))
    pairs.append(start(remote(pr.at[ghi], gpr.at[y, ghi], ysend.at[1, 4], yrecv.at[1, 4], left_y)))
    local = [
        pltpu.make_async_copy(pv.at[:, :, left_part], gpl.at[y], lsem.at[2]),
        pltpu.make_async_copy(pr, gpr.at[y], lsem.at[3]),
        pltpu.make_async_copy(meta, gmeta.at[y], lsem.at[4]),
    ]
    for copy in local:
        copy.start()

    def forward_z(k, q):
        for side, hops, device in ((0, NZ - k, right_z), (1, k, left_z)):
            slot = ((z + hops) % NZ) * NC + c
            part = q if side == 0 else 1 - q
            rs = pl.ds(part * half, half)
            line = zr if side == 0 else zl
            line[2 * (k - 1) + q].wait_recv()
            block = gi.at[slot, rs]
            if k < 3 or (k == 3 and q == 0):
                start(remote(block, block, zsend.at[side, 2 * k + q], zrecv.at[side, 2 * k + q], device), line)
            n = len(dd)
            start(remote(block, block, dsend.at[n], drecv.at[n], sibling), dd)

    mask_up[...], mask_dn[...] = row_masks(t)
    edge = jnp.zeros((PAD, 128), jnp.float32)
    for s in range(NP):
        for comp in range(3):
            for n in range(TILES_X):
                net[s, comp, n, 0:PAD, :] = edge
                net[s, comp, n, HIGH - PAD :, :] = edge
    middle = pl.ds(PAD + HALO, ROWS)

    def begin():
        for copy in meshes:
            copy.wait_recv()
        net[p, :, :, middle, :] = own[...]

        @pl.loop(0, HIGH // 8)
        def _(b):
            here = pl.ds(pl.multiple_of(b * 8, 8), 8)
            values = net[:, 0:2, :, here, :]
            uu[0, :, :, :, here, :] = values
            uu[1, :, :, :, here, :] = values
            vel[:, :, :, here, :] = jnp.zeros_like(values)

    def relax(first, count):
        edge = first // 8

        @pl.loop(first, first + count)
        def _(step):
            @pl.loop(PAD // 8 + edge, (HIGH - PAD) // 8 - edge)
            def _(b):
                relax_block(
                    net, uu.at[step % 2], uu.at[(step + 1) % 2], vel,
                    lambda s, n, here: net[s, 2, n, here, :], mask_up, mask_dn,
                    pl.multiple_of(b * 8, 8), TILES_X,
                )

    forward_z(1, 0)
    forward_z(1, 1)
    begin()
    relax(0, 4)
    forward_z(2, 0)
    relax(4, 4)
    yr[0].wait_recv()
    yl[0].wait_recv()
    pairs[0].wait_recv()
    pairs[1].wait_recv()
    before, after = (y + NY - 1) % NY, (y + 1) % NY
    far = []
    for side, first, which, groups, device in ((0, before, hi, ghi, right_y), (1, after, lo, glo, left_y)):
        block = gpl.at[first, which]
        start(remote(block, block, ysend.at[side, 2], yrecv.at[side, 2], device), far)
        block = gpr.at[first, groups]
        start(remote(block, block, ysend.at[side, 5], yrecv.at[side, 5], device), far)
    forward_z(2, 1)
    relax(8, 4)
    forward_z(3, 0)
    relax(12, 4)
    forward_z(3, 1)
    relax(16, 4)
    forward_z(4, 0)
    relax(20, 12)

    for n in range(TILES_X):
        moved = jnp.zeros((2, ROWS, 128), jnp.float32)
        for s in range(NP):
            moved = jnp.where(p == s, uu[0, s, :, n, middle, :], moved)
        u_own[:, :, 128 * n : 128 * n + 128] = moved
    lane = lax.broadcasted_iota(jnp.int32, (SPAN, 128), 1)
    for s in range(NP):
        parts = [net[s, 2, n, PAD : PAD + SPAN, :] for n in range(4)]
        low = jnp.where(lane < 32, pltpu.roll(parts[0], 32, axis=1), pltpu.roll(parts[1], 32, axis=1))
        top = jnp.where(lane < 96, pltpu.roll(parts[2], 96, axis=1), pltpu.roll(parts[3], 96, axis=1))
        mob_band[s] = jnp.where(lane < 64, low, top)

    for copy in yr[1:] + yl[1:] + pairs[2:] + far + metas + dd:
        copy.wait_recv()
    for copy in sent:
        copy.wait_send()
    for copy in local:
        copy.wait()
    keep.wait()


def flow_kernel(
    meta, gi, gpl, gpr, rows_tab, cols_tab, quads_tab, inv_left, inv_right, out,
    items, xbuf, mbuf, sum_e, sum_r, sems,
):
    _, y, _, _ = my_place()

    def note(n, count):
        h, j = n // PATCH_DEV, n % PATCH_DEV
        items[count] = n
        return count + (meta[h, 0, j] // (NZ * NC) == y).astype(jnp.int32)

    count = lax.fori_loop(0, NY * PATCH_DEV, note, jnp.int32(0))
    sum_e[...] = jnp.zeros_like(sum_e)
    sum_r[...] = jnp.zeros_like(sum_r)
    rounds = (count + GROUP - 1) // GROUP

    def item(step, g):
        n = items[jnp.minimum(step * GROUP + g, count - 1)]
        return n // PATCH_DEV, n % PATCH_DEV

    def place(h, j):
        first_row, first_col = meta[h, 1, j], meta[h, 2, j]
        row = jnp.minimum(first_row // 16 * 16, TILE - WIN_ROWS)
        col = jnp.where(first_col >= 128, 128, 0)
        return row, first_row - row, col, first_col - col

    def copies(step, slot, g):
        h, j = item(step, g)
        row, _, col, _ = place(h, j)
        window = gi.at[
            meta[h, 0, j] % (NZ * NC),
            pl.ds(pl.multiple_of(row, 16), WIN_ROWS),
            pl.ds(pl.multiple_of(col, 128), WIN_COLS),
        ]
        return (
            pltpu.make_async_copy(window, xbuf.at[slot, g], sems.at[slot, g, 0]),
            pltpu.make_async_copy(gpl.at[h, j], mbuf.at[slot, g, :, pl.ds(0, 128)], sems.at[slot, g, 1]),
            pltpu.make_async_copy(gpr.at[h, j // 4], mbuf.at[slot, g, :, pl.ds(128, 128)], sems.at[slot, g, 2]),
        )

    def fetch(step, slot):
        for g in range(GROUP):
            for copy in copies(step, slot, g):
                copy.start()

    def dot(a, b):
        return jnp.dot(a, b, preferred_element_type=jnp.float32)

    signed = lax.broadcasted_iota(jnp.int32, (W, 256), 0)
    signed = jnp.where(signed < W // 2, signed, signed - W).astype(jnp.float32)

    def work(step, slot):
        results = []
        for g in range(GROUP):
            h, j = item(step, g)
            _, row_shift, _, col_shift = place(h, j)
            cut = pl.ds(MAX_SHIFT - col_shift, WIN_COLS)
            columns = jnp.concatenate([cols_tab[0, cut, :], cols_tab[1, cut, :]], axis=1).astype(jnp.bfloat16)
            fixed = dot(xbuf[slot, g], columns).astype(jnp.bfloat16)
            fixed = dot(rows_tab[row_shift], fixed)
            moving = dot(mbuf[slot, g], quads_tab[j % 4]).astype(jnp.bfloat16)
            moving = dot(rows_tab[0, :, 0:W], moving)
            fcc, fcs, fsc, fss = fixed[:BLK, :128], fixed[:BLK, 128:], fixed[BLK:, :128], fixed[BLK:, 128:]
            mcc, mcs, msc, mss = moving[:BLK, :128], moving[:BLK, 128:], moving[BLK:, :128], moving[BLK:, 128:]
            ee = fcc * mcc + fss * mss + fcs * mcs + fsc * msc
            oo = fcc * mss + fss * mcc - fcs * msc - fsc * mcs
            eo = fcc * mcs - fcs * mcc + fsc * mss - fss * msc
            oe = fcc * msc - fsc * mcc + fcs * mss - fss * mcs
            cross = jnp.concatenate(
                [jnp.concatenate([ee, eo], axis=1), jnp.concatenate([oe, oo], axis=1)], axis=0
            ).astype(jnp.bfloat16)
            back = dot(inv_left[...], cross).astype(jnp.bfloat16)
            corr = dot(back, inv_right[...])
            energy = corr * corr
            at = h * PATCH_DEV + j % 2 * ROWS + j // 2
            results.append(
                (at, jnp.sum(energy, axis=0, keepdims=True), jnp.sum(energy * signed, axis=0, keepdims=True))
            )
        for at, plain, by_row in results:
            sum_e[pl.ds(at, 1), :] = plain
            sum_r[pl.ds(at, 1), :] = by_row

    @pl.when(rounds > 0)
    def _():
        fetch(0, 0)

    def one(step, carry):
        slot = step % DEPTH

        @pl.when(step + 1 < rounds)
        def _():
            fetch(step + 1, (step + 1) % DEPTH)

        for g in range(GROUP):
            for copy in copies(step, slot, g):
                copy.wait()
        work(step, slot)
        return carry

    lax.fori_loop(0, rounds, one, 0)

    number = lax.broadcasted_iota(jnp.int32, (NY * PATCH_DEV, 256), 1)
    shift = jnp.where(number < W // 2, number, number - W).astype(jnp.float32)
    plain = sum_e[...]
    total = jnp.sum(plain, axis=1, keepdims=True) + EPS
    flows = (
        jnp.sum(sum_r[...], axis=1, keepdims=True) / total,
        jnp.sum(plain * shift, axis=1, keepdims=True) / total,
    )
    lane = lax.broadcasted_iota(jnp.int32, (ROWS, 128), 1)
    for h in range(NY):
        block = jnp.zeros((ROWS, 128), jnp.float32)
        for comp in range(2):
            for side in range(2):
                first = h * PATCH_DEV + side * ROWS
                block = jnp.where(lane == 32 + 64 * side + comp, flows[comp][first : first + ROWS], block)
        out[h] = block


def share_kernel(ep, net, got, total, fsend, frecv, hsend, hrecv, lsem):
    t, y, z, c = my_place()
    p = lax.axis_index("pair")
    homes = [device_at((y + d) % NY, z, c) for d in range(1, NY)]
    halo = list(halo_targets(t, p))
    greet(homes + [device for _, _, device in halo])
    first = []
    for n, device in enumerate(homes):
        copy = remote(ep.at[(y + n + 1) % NY], got.at[n], fsend.at[n], frecv.at[n], device)
        copy.start()
        first.append(copy)
    for copy in first:
        copy.wait_recv()
    total[...] = ep[y] + got[0] + got[1] + got[2]
    second = []
    for n, (dp, d, device) in enumerate(halo):
        copy = remote(total, net.at[p, pl.ds(ROWS * (2 - d), ROWS), :], hsend.at[n], hrecv.at[n], device)
        copy.start()
        second.append(copy)
    own = pltpu.make_async_copy(total, net.at[p, pl.ds(HALO, ROWS), :], lsem)
    own.start()
    for copy in second:
        copy.wait_recv()
    for copy in first + second:
        copy.wait_send()
    own.wait()


def settle_kernel(net, mob_band, u_own, flow, out, tgt, mob, ua, ub, vel, mask_up, mask_dn):
    t = lax.axis_index("tile")
    p = lax.axis_index("pair")
    mask_up[...], mask_dn[...] = row_masks(t)
    lane = lax.broadcasted_iota(jnp.int32, (SPAN, 128), 1)
    node = (lane == 32) | (lane == 96)
    edge = jnp.zeros((PAD, 128), jnp.float32)
    span = pl.ds(PAD, SPAN)
    vel[...] = jnp.zeros_like(vel)
    ua[...] = jnp.zeros_like(ua)
    ub[...] = jnp.zeros_like(ub)
    for s in range(NP):
        values = net[s]
        for comp in range(2):
            turned = values if comp == 0 else pltpu.roll(values, 127, axis=1)
            tgt[s, comp, 0, span, :] = jnp.where(node, turned, 0.0)
        mob[s, span, :] = mob_band[s]
        mob[s, 0:PAD, :] = edge
        mob[s, HIGH - PAD :, :] = edge

    for first in range(0, STEPS, 8):

        @pl.loop(0, 4)
        def _(_):
            for u_in, u_out in ((ua, ub), (ub, ua)):
                for rows in range(PAD + first, HIGH - PAD - first, 8):
                    relax_block(
                        tgt, u_in, u_out, vel, lambda s, n, here: mob[s, here, :], mask_up, mask_dn, rows, 1
                    )

    middle = pl.ds(PAD + HALO, ROWS)
    lane = lax.broadcasted_iota(jnp.int32, (ROWS, 128), 1)
    row = lax.broadcasted_iota(jnp.int32, (ROWS, 128), 0)
    for comp in range(2):
        moved = jnp.zeros((ROWS, 128), jnp.float32)
        given = jnp.zeros((ROWS, 128), jnp.float32)
        for s in range(NP):
            moved = jnp.where(p == s, ua[s, comp, 0, middle, :], moved)
            given = jnp.where(p == s, tgt[s, comp, 0, middle, :], given)
        wide, narrow = pltpu.roll(moved, 96, axis=1), pltpu.roll(moved, 32, axis=1)
        for n, (part, inside) in enumerate(((wide, lane >= 96), (wide, lane < 32), (narrow, lane >= 96), (narrow, lane < 32))):
            columns = pl.ds(128 * n, 128)
            out[comp, :, columns] = u_own[comp, :, columns] + jnp.where(inside, part, 0.0)
        even = jnp.sum(jnp.where(lane == 32, given, 0.0), axis=1, keepdims=True)
        odd = jnp.sum(jnp.where(lane == 96, given, 0.0), axis=1, keepdims=True)
        spread = jnp.where(lane == 2 * row, even, 0.0) + jnp.where(lane == 2 * row + 1, odd, 0.0)
        flow[comp : comp + 1, :] = jnp.sum(spread, axis=0, keepdims=True)[:, :PATCH_DEV]


def make_tables():
    numbers = np.arange(W)
    phase = (numbers[:, None] * numbers[None, :] % W).astype(np.float32) * np.float32(2.0 * math.pi / W)
    scale = np.float32(1.0 / math.sqrt(W))
    cos = (np.cos(phase) * scale).astype(ml_dtypes.bfloat16).astype(np.float32)
    sin = (np.sin(phase) * scale).astype(ml_dtypes.bfloat16).astype(np.float32)
    left = np.zeros((FREQ, W), np.float32)
    left[:HALF], left[BLK : BLK + HALF] = cos[:HALF], sin[:HALF]
    right = np.zeros((W, 256), np.float32)
    right[:, :HALF], right[:, 128 : 128 + HALF] = cos[:, :HALF], sin[:, :HALF]
    rows_tab = np.zeros((17, FREQ, WIN_ROWS), np.float32)
    for shift in range(17):
        rows_tab[shift, :, shift : shift + W] = left
    cols_tab = np.zeros((2, MAX_SHIFT + WIN_COLS, 128), np.float32)
    cols_tab[0, MAX_SHIFT : MAX_SHIFT + W] = right[:, :128]
    cols_tab[1, MAX_SHIFT : MAX_SHIFT + W] = right[:, 128:]
    quads_tab = np.zeros((4, 256, 256), np.float32)
    for q in range(4):
        quads_tab[q, :128] = right[:128]
        quads_tab[q, 128 + 32 * q : 160 + 32 * q] = right[128:]
    weight = np.full((HALF, 1), 2.0, np.float32)
    weight[0] = weight[-1] = 1.0
    inv_left = np.zeros((W, FREQ), np.float32)
    inv_left[:, :HALF], inv_left[:, BLK : BLK + HALF] = (weight * cos[:HALF]).T, (-2.0 * sin[:HALF]).T
    inv_right = np.zeros((256, 256), np.float32)
    inv_right[:HALF, :W], inv_right[128 : 128 + HALF, :W] = weight * cos[:HALF], -2.0 * sin[:HALF]
    half = lambda table: table.astype(ml_dtypes.bfloat16)
    return half(rows_tab), cols_tab, half(quads_tab), half(inv_left), half(inv_right)


def any_spec():
    return pl.BlockSpec(memory_space=pl.ANY)


def vmem_spec():
    return pl.BlockSpec(memory_space=pltpu.VMEM)


def shards(fixed_image, moving_patches, owners, offsets, mobility, prior_flow):
    meta = jnp.pad(jnp.concatenate([owners, offsets[0].T], axis=0), ((0, 5), (0, 96)))
    f32, bf16 = jnp.float32, jnp.bfloat16
    sds = jax.ShapeDtypeStruct
    dma = pltpu.SemaphoreType.DMA
    gi, gpl, gpr, gmeta, u_own, mob_band = pl.pallas_call(
        gather_kernel,
        out_shape=(
            sds((NZ * NC, TILE, TILE), bf16),
            sds((NY, PATCH_DEV, W, 128), bf16),
            sds((NY, PATCH_DEV // 4, W, 128), bf16),
            sds((NY, 8, 128), jnp.int32),
            sds((2, ROWS, COLS), f32),
            sds((NP, SPAN, 128), f32),
        ),
        in_specs=[any_spec(), any_spec(), vmem_spec(), vmem_spec(), vmem_spec()],
        out_specs=(any_spec(), any_spec(), any_spec(), any_spec(), vmem_spec(), vmem_spec()),
        scratch_shapes=[
            pltpu.VMEM((PATCH_DEV, W, W), bf16),
            pltpu.VMEM((PATCH_DEV // 4, W, 128), bf16),
            pltpu.VMEM((3, TILES_X, ROWS, 128), f32),
            pltpu.VMEM((NP, 3, TILES_X, HIGH, 128), f32),
            pltpu.VMEM((2, NP, 2, TILES_X, HIGH, 128), f32),
            pltpu.VMEM((NP, 2, TILES_X, HIGH, 128), f32),
            pltpu.VMEM((HIGH, 128), f32),
            pltpu.VMEM((HIGH, 128), f32),
            dma((5,)), dma((2, 6)), dma((2, 6)), dma((2, 8)), dma((2, 8)), dma((16,)), dma((16,)),
            dma((3,)), dma((3,)), dma((19,)), dma((19,)),
        ],
        compiler_params=pltpu.CompilerParams(
            collective_id=0, has_side_effects=True, vmem_limit_bytes=32 * 2**20
        ),
        name="gather_and_relax",
    )(fixed_image[0], moving_patches[0], meta, prior_flow[0], mobility[0])
    tables = [jnp.asarray(table) for table in make_tables()]
    ep = pl.pallas_call(
        flow_kernel,
        out_shape=sds((NY, ROWS, 128), f32),
        in_specs=[pl.BlockSpec(memory_space=pltpu.SMEM)] + [any_spec()] * 3 + [vmem_spec()] * 5,
        out_specs=vmem_spec(),
        scratch_shapes=[
            pltpu.SMEM((NY * PATCH_DEV + 1,), jnp.int32),
            pltpu.VMEM((DEPTH, GROUP, WIN_ROWS, WIN_COLS), bf16),
            pltpu.VMEM((DEPTH, GROUP, W, 256), bf16),
            pltpu.VMEM((NY * PATCH_DEV, 256), f32),
            pltpu.VMEM((NY * PATCH_DEV, 256), f32),
            dma((DEPTH, GROUP, 3)),
        ],
        compiler_params=pltpu.CompilerParams(vmem_limit_bytes=32 * 2**20),
        name="patch_flows",
    )(gmeta, gi, gpl, gpr, *tables)
    net = pl.pallas_call(
        share_kernel,
        out_shape=sds((NP, SPAN, 128), f32),
        in_specs=[vmem_spec()],
        out_specs=any_spec(),
        scratch_shapes=[
            pltpu.VMEM((3, ROWS, 128), f32), pltpu.VMEM((ROWS, 128), f32),
            dma((3,)), dma((3,)), dma((19,)), dma((19,)), dma(()),
        ],
        compiler_params=pltpu.CompilerParams(collective_id=1, has_side_effects=True),
        name="share_flows",
    )(ep)
    flow, out = pl.pallas_call(
        settle_kernel,
        out_shape=(sds((2, PATCH_DEV), f32), sds((2, ROWS, COLS), f32)),
        in_specs=[vmem_spec()] * 3,
        out_specs=(vmem_spec(), vmem_spec()),
        scratch_shapes=[
            pltpu.VMEM((NP, 2, 1, HIGH, 128), f32),
            pltpu.VMEM((NP, HIGH, 128), f32),
            pltpu.VMEM((NP, 2, 1, HIGH, 128), f32),
            pltpu.VMEM((NP, 2, 1, HIGH, 128), f32),
            pltpu.VMEM((NP, 2, 1, HIGH, 128), f32),
            pltpu.VMEM((HIGH, 128), f32),
            pltpu.VMEM((HIGH, 128), f32),
        ],
        compiler_params=pltpu.CompilerParams(vmem_limit_bytes=32 * 2**20),
        name="settle",
    )(net, mob_band, u_own)
    return flow[None], out[None]


def solution(mesh):
    in_specs = (
        P("pair", "tile", None),
        P("pair", "tile", None, None),
        P("pair", "tile"),
        P("pair", "tile", None),
        P("pair", "tile", None),
        P("pair", None, "tile", None),
    )
    out_specs = (P("pair", None, "tile"), P("pair", None, "tile", None))
    return jax.shard_map(shards, mesh=mesh, in_specs=in_specs, out_specs=out_specs, check_vma=False)
```

```python
import functools
import math

import jax
import jax.numpy as jnp
import ml_dtypes
import numpy as np
from jax import lax
from jax.experimental import pallas as pl
from jax.experimental.pallas import tpu as pltpu
from jax.sharding import PartitionSpec as P

MESH = pl.DeviceIdType.MESH
NY, NZ, NC, NP = 4, 8, 2, 4
TILES = NY * NZ * NC
W = 160
TILE = 512
PATCH_DEV = 32
STEPS = 32
EPS = 1e-06
ROWS = 16
COLS = 512
TILES_X = COLS // 128
HALO = 32
PAD = 8
SPAN = ROWS + 2 * HALO
HIGH = SPAN + 2 * PAD
HALF = W // 2 + 1
BLK = 88
FREQ = 2 * BLK
WIN_ROWS = 176
WIN_COLS = 384
GROUP = 8
DEPTH = 2


def device_at(y, z, c):
    return {"tile": (y * NZ + z) * NC + c}


def my_place():
    t = lax.axis_index("tile")
    return t, t // (NZ * NC), (t // NC) % NZ, t % NC


def halo_targets(t, p):
    for dp in range(NP):
        for d in range(-2, 3):
            if dp or d:
                there = {"tile": (t + d + TILES) % TILES, "pair": (p + dp) % NP}
                yield dp, d, there


def remote(src, dst, send, recv, device):
    return pltpu.make_async_remote_copy(
        src_ref=src, dst_ref=dst, send_sem=send, recv_sem=recv, device_id=device, device_id_type=MESH
    )


def greet(devices):
    barrier = pltpu.get_barrier_semaphore()
    for device in devices:
        pl.semaphore_signal(barrier, inc=1, device_id=device, device_id_type=MESH)
    pl.semaphore_wait(barrier, len(devices))


def relax_step(t, target, u_in, u_out, vel, mob, first, last, tiles):
    shape = (NP, tiles, 8, 128)
    lane = lax.broadcasted_iota(jnp.int32, shape, 3)
    line = lax.broadcasted_iota(jnp.int32, shape, 2)
    own = PAD + HALO
    for rows in range(first, last, 8):
        here = pl.ds(rows, 8)
        for comp in range(2):
            u = u_in[:, comp, :, here, :]
            above = u_in[:, comp, :, pl.ds(rows - 1, 8), :]
            below = u_in[:, comp, :, pl.ds(rows + 1, 8), :]
            if rows in (own, own - ROWS):
                above = jnp.where((line == 0) & (t == (own - rows) // ROWS), u, above)
            if rows + 8 in (own + ROWS, own + 2 * ROWS):
                below = jnp.where((line == 7) & (t == TILES - (rows + 8 - own) // ROWS), u, below)
            left, right = pltpu.roll(u, 1, axis=3), pltpu.roll(u, 127, axis=3)
            if tiles > 1:
                left = jnp.where(lane == 0, jnp.concatenate([u[:, :1], left[:, :-1]], axis=1), left)
                right = jnp.where(lane == 127, jnp.concatenate([right[:, 1:], u[:, -1:]], axis=1), right)
            inter = jnp.concatenate([u[:1], u[:-1]], axis=0) + jnp.concatenate([u[1:], u[-1:]], axis=0)
            force = ((above + below) + (left + right)) + (0.2 / 0.35) * inter
            force = force + target[:, comp, :, here, :] - (4.0 + 0.7 / 0.35) * u
            speed = 0.8 * vel[:, comp, :, here, :] + mob(here) * force
            vel[:, comp, :, here, :] = speed
            u_out[:, comp, :, here, :] = u + speed


def gather_kernel(
    img, pat, meta, prior, mob, gi, gpl, gpr, gmeta, u_own, mob_band,
    pv, pr, own, net, target, ua, ub, vel,
    lsem, ysend, yrecv, zsend, zrecv, dsend, drecv, msend, mrecv, hsend, hrecv,
):
    t, y, z, c = my_place()
    p = lax.axis_index("pair")
    right_y, left_y = device_at((y + 1) % NY, z, c), device_at((y + NY - 1) % NY, z, c)
    right_z, left_z = device_at(y, (z + 1) % NZ, c), device_at(y, (z + NZ - 1) % NZ, c)
    across_y = device_at((y + 2) % NY, z, c)
    sibling = device_at(y, z, 1 - c)
    stage = pltpu.make_async_copy(pat, pv, lsem.at[0])
    stage.start()
    mine = z * NC + c
    keep = pltpu.make_async_copy(img, gi.at[mine], lsem.at[1])
    keep.start()
    halo = list(halo_targets(t, p))
    greet([right_y, left_y, across_y, right_z, left_z, sibling] + [device for _, _, device in halo])

    lo, hi = pl.ds(0, 16), pl.ds(16, 16)
    glo, ghi = pl.ds(0, 4), pl.ds(4, 4)
    left_part = pl.ds(0, 128)
    sent = []
    yr, yl = [], []

    def start(copy, into=None):
        copy.start()
        sent.append(copy)
        if into is not None:
            into.append(copy)
        return copy

    def y_left(which, first, side, device, slot):
        return remote(
            pat.at[which, :, left_part], gpl.at[first, which], ysend.at[side, slot], yrecv.at[side, slot], device
        )

    start(y_left(hi, y, 0, right_y, 0), yr)
    start(y_left(lo, y, 1, left_y, 0), yl)

    for n in range(TILES_X):
        columns = pl.ds(128 * n, 128)
        own[0:2, n] = prior[:, :, columns].astype(jnp.bfloat16)
        own[2, n] = mob[:, columns].astype(jnp.bfloat16)
    meshes = []
    for n, (dp, d, device) in enumerate(halo):
        rows = pl.ds(ROWS * (2 - d), ROWS)
        copy = remote(own, net.at[p, :, :, rows, :], hsend.at[n], hrecv.at[n], device)
        start(copy, meshes)

    half = TILE // 2
    zr, zl, dd = [], [], []
    for q in range(2):
        rs = pl.ds(q * half, half)
        start(remote(img.at[rs], gi.at[mine, rs], zsend.at[0, q], zrecv.at[0, q], right_z), zr)
        rs = pl.ds((1 - q) * half, half)
        start(remote(img.at[rs], gi.at[mine, rs], zsend.at[1, q], zrecv.at[1, q], left_z), zl)
    start(y_left(lo, y, 0, right_y, 1), yr)
    start(y_left(hi, y, 1, left_y, 1), yl)
    metas = []
    for n, device in enumerate((right_y, left_y, across_y)):
        start(remote(meta, gmeta.at[y], msend.at[n], mrecv.at[n], device), metas)
    start(remote(img, gi.at[mine], dsend.at[0], drecv.at[0], sibling), dd)

    stage.wait()
    for g in range(PATCH_DEV // 4):
        pr[g] = jnp.concatenate([pv[4 * g + q, :, 128:W] for q in range(4)], axis=1)
    pairs = []
    pairs.append(start(remote(pr.at[ghi], gpr.at[y, ghi], ysend.at[0, 3], yrecv.at[0, 3], right_y)))
    pairs.append(start(remote(pr.at[glo], gpr.at[y, glo], ysend.at[1, 3], yrecv.at[1, 3], left_y)))
    pairs.append(start(remote(pr.at[glo], gpr.at[y, glo], ysend.at[0, 4], yrecv.at[0, 4], right_y)))
    pairs.append(start(remote(pr.at[ghi], gpr.at[y, ghi], ysend.at[1, 4], yrecv.at[1, 4], left_y)))
    local = [
        pltpu.make_async_copy(pv.at[:, :, left_part], gpl.at[y], lsem.at[2]),
        pltpu.make_async_copy(pr, gpr.at[y], lsem.at[3]),
        pltpu.make_async_copy(meta, gmeta.at[y], lsem.at[4]),
    ]
    for copy in local:
        copy.start()

    def forward_z(k, q):
        for side, hops, device in ((0, NZ - k, right_z), (1, k, left_z)):
            slot = ((z + hops) % NZ) * NC + c
            part = q if side == 0 else 1 - q
            rs = pl.ds(part * half, half)
            line = zr if side == 0 else zl
            line[2 * (k - 1) + q].wait_recv()
            block = gi.at[slot, rs]
            if k < 3 or (k == 3 and q == 0):
                start(remote(block, block, zsend.at[side, 2 * k + q], zrecv.at[side, 2 * k + q], device), line)
            n = len(dd)
            start(remote(block, block, dsend.at[n], drecv.at[n], sibling), dd)

    middle = pl.ds(PAD + HALO, ROWS)

    def begin():
        for copy in meshes:
            copy.wait_recv()
        net[p, :, :, HALO : HALO + ROWS, :] = own[...]
        edge = jnp.zeros((NP, 2, TILES_X, PAD, 128), jnp.float32)
        for ref in (ua, ub):
            ref[:, :, :, 0:PAD, :] = edge
            ref[:, :, :, HIGH - PAD :, :] = edge

        @pl.loop(0, NP)
        def _(s):
            for b in range(SPAN // ROWS):
                rows = pl.ds(PAD + ROWS * b, ROWS)
                values = net[s, :, :, ROWS * b : ROWS * b + ROWS, :].astype(jnp.float32)
                ua[s, :, :, rows, :] = values[0:2]
                ub[s, :, :, rows, :] = values[0:2]
                vel[s, :, :, rows, :] = jnp.zeros_like(values[0:2])
                target[s, 0:2, :, rows, :] = (0.3 / 0.35) * values[0:2]
                target[s, 2, :, rows, :] = 0.35 * values[2]

        for n in range(TILES_X):
            columns = pl.ds(128 * n, 128)
            values = prior[:, :, columns]
            ua[p, :, n, middle, :] = values
            target[p, 0:2, n, middle, :] = (0.3 / 0.35) * values
            target[p, 2, n, middle, :] = 0.35 * mob[:, columns]

    def relax(first):
        @pl.loop(0, 4)
        def _(_):
            for u_in, u_out in ((ua, ub), (ub, ua)):
                relax_step(
                    t, target, u_in, u_out, vel, lambda here: target[:, 2, :, here, :],
                    PAD + first, HIGH - PAD - first, TILES_X,
                )

    forward_z(1, 0)
    forward_z(1, 1)
    begin()
    relax(0)
    forward_z(2, 0)
    yr[0].wait_recv()
    yl[0].wait_recv()
    pairs[0].wait_recv()
    pairs[1].wait_recv()
    before, after = (y + NY - 1) % NY, (y + 1) % NY
    far = []
    for side, first, which, groups, device in ((0, before, hi, ghi, right_y), (1, after, lo, glo, left_y)):
        block = gpl.at[first, which]
        start(remote(block, block, ysend.at[side, 2], yrecv.at[side, 2], device), far)
        block = gpr.at[first, groups]
        start(remote(block, block, ysend.at[side, 5], yrecv.at[side, 5], device), far)
    relax(8)
    forward_z(2, 1)
    relax(16)
    forward_z(3, 0)
    relax(24)
    forward_z(3, 1)
    forward_z(4, 0)

    for n in range(TILES_X):
        moved = jnp.zeros((2, ROWS, 128), jnp.float32)
        for s in range(NP):
            moved = jnp.where(p == s, ua[s, :, n, middle, :], moved)
        u_own[:, :, 128 * n : 128 * n + 128] = moved
    lane = lax.broadcasted_iota(jnp.int32, (SPAN, 128), 1)
    for s in range(NP):
        parts = [target[s, 2, n, PAD : PAD + SPAN, :] for n in range(4)]
        low = jnp.where(lane < 32, pltpu.roll(parts[0], 32, axis=1), pltpu.roll(parts[1], 32, axis=1))
        top = jnp.where(lane < 96, pltpu.roll(parts[2], 96, axis=1), pltpu.roll(parts[3], 96, axis=1))
        mob_band[s] = jnp.where(lane < 64, low, top)

    for copy in yr[1:] + yl[1:] + pairs[2:] + far + metas + dd:
        copy.wait_recv()
    for copy in sent:
        copy.wait_send()
    for copy in local:
        copy.wait()
    keep.wait()


def flow_kernel(
    meta, gi, gpl, gpr, rows_hbm, cols_hbm, left_hbm, right_hbm, out,
    items, rows_tab, cols_tab, inv_left, inv_right, xbuf, mbuf, lines, halves, backs, sum_e, sum_r, sems, tsems,
):
    _, y, _, _ = my_place()
    tables = [
        pltpu.make_async_copy(src, dst, tsems.at[n])
        for n, (src, dst) in enumerate(
            ((cols_hbm, cols_tab), (rows_hbm, rows_tab), (left_hbm, inv_left), (right_hbm, inv_right))
        )
    ]

    def note(h, count):
        for j in range(PATCH_DEV):
            items[count] = h * PATCH_DEV + j
            count = count + (meta[h, 0, j] // (NZ * NC) == y).astype(jnp.int32)
        return count

    count = lax.fori_loop(0, NY, note, jnp.int32(0))
    sum_e[...] = jnp.zeros_like(sum_e)
    sum_r[...] = jnp.zeros_like(sum_r)
    rounds = (count + GROUP - 1) // GROUP

    def item(step, g):
        n = items[jnp.minimum(step * GROUP + g, count - 1)]
        return n // PATCH_DEV, n % PATCH_DEV

    def place(h, j):
        first_row, first_col = meta[h, 1, j], meta[h, 2, j]
        row = jnp.minimum(first_row // 16 * 16, TILE - WIN_ROWS)
        col = first_col // 128 * 128
        return row, first_row - row, col, first_col - col

    def copies(step, slot, g):
        h, j = item(step, g)
        row, _, col, _ = place(h, j)
        image = gi.at[meta[h, 0, j] % (NZ * NC)]
        rows = pl.ds(pl.multiple_of(row, 16), WIN_ROWS)
        third = jnp.minimum(col + 256, TILE - 128)
        pieces = (
            (image.at[rows, pl.ds(pl.multiple_of(col, 128), 256)], xbuf.at[slot, g, :, pl.ds(0, 256)]),
            (image.at[rows, pl.ds(pl.multiple_of(third, 128), 128)], xbuf.at[slot, g, :, pl.ds(256, 128)]),
            (gpl.at[h, j], mbuf.at[slot, g, :, pl.ds(0, 128)]),
            (gpr.at[h, j // 4], mbuf.at[slot, g, :, pl.ds(128, 128)]),
        )
        return [pltpu.make_async_copy(src, dst, sems.at[slot, g, n]) for n, (src, dst) in enumerate(pieces)]

    def fetch(step, slot):
        for g in range(GROUP):
            for copy in copies(step, slot, g):
                copy.start()

    def dot(a, b):
        return jnp.dot(a, b, preferred_element_type=jnp.float32)

    signed = lax.broadcasted_iota(jnp.int32, (W, 256), 0)
    signed = jnp.where(signed < W // 2, signed, signed - W).astype(jnp.float32)
    win_lane = lax.broadcasted_iota(jnp.int32, (WIN_ROWS, 128), 1)
    base = GROUP * WIN_ROWS

    def turn(x, amount):
        return pltpu.roll(x.astype(jnp.float32), (128 - amount) % 128, axis=1)

    def work(step, slot):
        place_of = []
        for g in range(GROUP):
            h, j = item(step, g)
            _, row_shift, _, col_shift = place(h, j)
            place_of.append((h, j, row_shift))
            parts = [turn(xbuf[slot, g, :, 128 * n : 128 * n + 128], col_shift) for n in range(3)]
            inside = win_lane < 128 - col_shift
            rows = pl.ds(g * WIN_ROWS, WIN_ROWS)
            lines[rows, 0:128] = jnp.where(inside, parts[0], parts[1]).astype(jnp.bfloat16)
            lines[rows, 128:256] = jnp.where(inside, parts[1], parts[2]).astype(jnp.bfloat16)
            rows = pl.ds(base + g * W, W)
            lines[rows, 0:128] = mbuf[slot, g, :, 0:128]
            lines[rows, 128:256] = turn(mbuf[slot, g, :, 128:256], j % 4 * 32).astype(jnp.bfloat16)
        halves[...] = dot(lines[...], cols_tab[...]).astype(jnp.bfloat16)
        spectra = [
            (
                dot(rows_tab[place_of[g][2]], halves[pl.ds(g * WIN_ROWS, WIN_ROWS), :]),
                dot(rows_tab[0, :, 0:W], halves[pl.ds(base + g * W, W), :]),
            )
            for g in range(GROUP)
        ]
        crosses = []
        for g in range(GROUP):
            fixed, moving = spectra[g]
            fcc, fcs, fsc, fss = fixed[:BLK, :128], fixed[:BLK, 128:], fixed[BLK:, :128], fixed[BLK:, 128:]
            mcc, mcs, msc, mss = moving[:BLK, :128], moving[:BLK, 128:], moving[BLK:, :128], moving[BLK:, 128:]
            ee = fcc * mcc + fss * mss + fcs * mcs + fsc * msc
            oo = fcc * mss + fss * mcc - fcs * msc - fsc * mcs
            eo = fcc * mcs - fcs * mcc + fsc * mss - fss * msc
            oe = fcc * msc - fsc * mcc + fcs * mss - fss * mcs
            cross = jnp.concatenate(
                [jnp.concatenate([ee, eo], axis=1), jnp.concatenate([oe, oo], axis=1)], axis=0
            ).astype(jnp.bfloat16)
            crosses.append(cross)
        for g in range(GROUP):
            backs[pl.ds(g * W, W), :] = dot(inv_left[...], crosses[g]).astype(jnp.bfloat16)
        corr = dot(backs[...], inv_right[...])
        for g in range(GROUP):
            h, j, _ = place_of[g]
            energy = corr[g * W : g * W + W]
            energy = energy * energy
            at = pl.ds(h * PATCH_DEV + j % 2 * ROWS + j // 2, 1)
            sum_e[at, :] = jnp.sum(energy, axis=0, keepdims=True)
            sum_r[at, :] = jnp.sum(energy * signed, axis=0, keepdims=True)

    @pl.when(rounds > 0)
    def _():
        fetch(0, 0)

    for copy in tables:
        copy.start()
    def one(step, carry):
        slot = step % DEPTH

        @pl.when(step + 1 < rounds)
        def _():
            fetch(step + 1, (step + 1) % DEPTH)

        for g in range(GROUP):
            for copy in copies(step, slot, g):
                copy.wait()
        work(step, slot)
        return carry

    for copy in tables:
        copy.wait()
    lax.fori_loop(0, rounds, one, 0)

    number = lax.broadcasted_iota(jnp.int32, (NY * PATCH_DEV, 256), 1)
    shift = jnp.where(number < W // 2, number, number - W).astype(jnp.float32)
    plain = sum_e[...]
    total = jnp.sum(plain, axis=1, keepdims=True) + EPS
    flows = (
        jnp.sum(sum_r[...], axis=1, keepdims=True) / total,
        jnp.sum(plain * shift, axis=1, keepdims=True) / total,
    )
    lane = lax.broadcasted_iota(jnp.int32, (ROWS, 128), 1)
    for h in range(NY):
        block = jnp.zeros((ROWS, 128), jnp.float32)
        for comp in range(2):
            for side in range(2):
                first = h * PATCH_DEV + side * ROWS
                block = jnp.where(lane == 32 + 64 * side + comp, flows[comp][first : first + ROWS], block)
        out[h] = block


def share_kernel(ep, net, got, total, fsend, frecv, hsend, hrecv, lsem):
    t, y, z, c = my_place()
    p = lax.axis_index("pair")
    homes = [device_at((y + d) % NY, z, c) for d in range(1, NY)]
    halo = list(halo_targets(t, p))
    greet(homes + [device for _, _, device in halo])
    first = []
    for n, device in enumerate(homes):
        copy = remote(ep.at[(y + n + 1) % NY], got.at[n], fsend.at[n], frecv.at[n], device)
        copy.start()
        first.append(copy)
    for copy in first:
        copy.wait_recv()
    total[...] = ep[y] + got[0] + got[1] + got[2]
    second = []
    for n, (dp, d, device) in enumerate(halo):
        copy = remote(total, net.at[p, pl.ds(ROWS * (2 - d), ROWS), :], hsend.at[n], hrecv.at[n], device)
        copy.start()
        second.append(copy)
    own = pltpu.make_async_copy(total, net.at[p, pl.ds(HALO, ROWS), :], lsem)
    own.start()
    for copy in second:
        copy.wait_recv()
    for copy in first + second:
        copy.wait_send()
    own.wait()


def settle_kernel(net, mob_band, u_own, flow, out, tgt, mob, ua, ub, vel):
    t = lax.axis_index("tile")
    p = lax.axis_index("pair")
    lane = lax.broadcasted_iota(jnp.int32, (SPAN, 128), 1)
    node = (lane == 32) | (lane == 96)
    span = pl.ds(PAD, SPAN)
    vel[...] = jnp.zeros_like(vel)
    ua[...] = jnp.zeros_like(ua)
    ub[...] = jnp.zeros_like(ub)
    for s in range(NP):
        values = net[s]
        for comp in range(2):
            turned = values if comp == 0 else pltpu.roll(values, 127, axis=1)
            tgt[s, comp, 0, span, :] = (0.3 / 0.35) * jnp.where(node, turned, 0.0)
        mob[s, 0, span, :] = mob_band[s]

    for first in range(0, STEPS, 8):

        @pl.loop(0, 4)
        def _(_):
            for u_in, u_out in ((ua, ub), (ub, ua)):
                relax_step(
                    t, tgt, u_in, u_out, vel, lambda here: mob[:, :, here, :], PAD + first, HIGH - PAD - first, 1
                )

    middle = pl.ds(PAD + HALO, ROWS)
    lane = lax.broadcasted_iota(jnp.int32, (ROWS, 128), 1)
    row = lax.broadcasted_iota(jnp.int32, (ROWS, 128), 0)
    for comp in range(2):
        moved = jnp.zeros((ROWS, 128), jnp.float32)
        given = net[p, HALO : HALO + ROWS, :]
        for s in range(NP):
            moved = jnp.where(p == s, ua[s, comp, 0, middle, :], moved)
        wide, narrow = pltpu.roll(moved, 96, axis=1), pltpu.roll(moved, 32, axis=1)
        for n, (part, inside) in enumerate(((wide, lane >= 96), (wide, lane < 32), (narrow, lane >= 96), (narrow, lane < 32))):
            columns = pl.ds(128 * n, 128)
            out[comp, :, columns] = u_own[comp, :, columns] + jnp.where(inside, part, 0.0)
        even = jnp.sum(jnp.where(lane == 32 + comp, given, 0.0), axis=1, keepdims=True)
        odd = jnp.sum(jnp.where(lane == 96 + comp, given, 0.0), axis=1, keepdims=True)
        spread = jnp.where(lane == 2 * row, even, 0.0) + jnp.where(lane == 2 * row + 1, odd, 0.0)
        flow[comp : comp + 1, :] = jnp.sum(spread, axis=0, keepdims=True)[:, :PATCH_DEV]


def make_tables():
    numbers = np.arange(W)
    phase = (numbers[:, None] * numbers[None, :] % W).astype(np.float32) * np.float32(2.0 * math.pi / W)
    scale = np.float32(1.0 / math.sqrt(W))
    cos = (np.cos(phase) * scale).astype(ml_dtypes.bfloat16).astype(np.float32)
    sin = (np.sin(phase) * scale).astype(ml_dtypes.bfloat16).astype(np.float32)
    left = np.zeros((FREQ, W), np.float32)
    left[:HALF], left[BLK : BLK + HALF] = cos[:HALF], sin[:HALF]
    right = np.zeros((W, 256), np.float32)
    right[:, :HALF], right[:, 128 : 128 + HALF] = cos[:, :HALF], sin[:, :HALF]
    rows_tab = np.zeros((17, FREQ, WIN_ROWS), np.float32)
    for shift in range(17):
        rows_tab[shift, :, shift : shift + W] = left
    cols_tab = np.zeros((256, 256), np.float32)
    cols_tab[:W] = right
    weight = np.full((HALF, 1), 2.0, np.float32)
    weight[0] = weight[-1] = 1.0
    inv_left = np.zeros((W, FREQ), np.float32)
    inv_left[:, :HALF], inv_left[:, BLK : BLK + HALF] = (weight * cos[:HALF]).T, (-2.0 * sin[:HALF]).T
    inv_right = np.zeros((256, 256), np.float32)
    inv_right[:HALF, :W], inv_right[128 : 128 + HALF, :W] = weight * cos[:HALF], -2.0 * sin[:HALF]
    half = lambda table: table.astype(ml_dtypes.bfloat16)
    return half(rows_tab), half(cols_tab), half(inv_left), half(inv_right)


def any_spec():
    return pl.BlockSpec(memory_space=pl.ANY)


def vmem_spec():
    return pl.BlockSpec(memory_space=pltpu.VMEM)


def flow_call(gmeta, gi, gpl, gpr):
    f32, bf16 = jnp.float32, jnp.bfloat16
    tables = [jnp.asarray(table) for table in make_tables()]
    return pl.pallas_call(
        flow_kernel,
        out_shape=jax.ShapeDtypeStruct((NY, ROWS, 128), f32),
        in_specs=[pl.BlockSpec(memory_space=pltpu.SMEM)] + [any_spec()] * 7,
        out_specs=vmem_spec(),
        scratch_shapes=[
            pltpu.SMEM((NY * PATCH_DEV + 1,), jnp.int32),
            pltpu.VMEM((17, FREQ, WIN_ROWS), bf16),
            pltpu.VMEM((256, 256), bf16),
            pltpu.VMEM((W, FREQ), bf16),
            pltpu.VMEM((256, 256), bf16),
            pltpu.VMEM((DEPTH, GROUP, WIN_ROWS, WIN_COLS), bf16),
            pltpu.VMEM((DEPTH, GROUP, W, 256), bf16),
            pltpu.VMEM((GROUP * (WIN_ROWS + W), 256), bf16),
            pltpu.VMEM((GROUP * (WIN_ROWS + W), 256), bf16),
            pltpu.VMEM((GROUP * W, 256), bf16),
            pltpu.VMEM((NY * PATCH_DEV, 256), f32),
            pltpu.VMEM((NY * PATCH_DEV, 256), f32),
            pltpu.SemaphoreType.DMA((DEPTH, GROUP, 4)),
            pltpu.SemaphoreType.DMA((4,)),
        ],
        compiler_params=pltpu.CompilerParams(vmem_limit_bytes=32 * 2**20),
        name="patch_flows",
    )(gmeta, gi, gpl, gpr, *tables)


def shards(fixed_image, moving_patches, owners, offsets, mobility, prior_flow):
    meta = jnp.pad(jnp.concatenate([owners, offsets[0].T], axis=0), ((0, 5), (0, 96)))
    f32, bf16 = jnp.float32, jnp.bfloat16
    sds = jax.ShapeDtypeStruct
    dma = pltpu.SemaphoreType.DMA
    gi, gpl, gpr, gmeta, u_own, mob_band = pl.pallas_call(
        gather_kernel,
        out_shape=(
            sds((NZ * NC, TILE, TILE), bf16),
            sds((NY, PATCH_DEV, W, 128), bf16),
            sds((NY, PATCH_DEV // 4, W, 128), bf16),
            sds((NY, 8, 128), jnp.int32),
            sds((2, ROWS, COLS), f32),
            sds((NP, SPAN, 128), f32),
        ),
        in_specs=[any_spec(), any_spec(), vmem_spec(), vmem_spec(), vmem_spec()],
        out_specs=(any_spec(), any_spec(), any_spec(), any_spec(), vmem_spec(), vmem_spec()),
        scratch_shapes=[
            pltpu.VMEM((PATCH_DEV, W, W), bf16),
            pltpu.VMEM((PATCH_DEV // 4, W, 128), bf16),
            pltpu.VMEM((3, TILES_X, ROWS, 128), bf16),
            pltpu.VMEM((NP, 3, TILES_X, SPAN, 128), bf16),
            pltpu.VMEM((NP, 3, TILES_X, HIGH, 128), f32),
            pltpu.VMEM((NP, 2, TILES_X, HIGH, 128), f32),
            pltpu.VMEM((NP, 2, TILES_X, HIGH, 128), f32),
            pltpu.VMEM((NP, 2, TILES_X, HIGH, 128), f32),
            dma((5,)), dma((2, 6)), dma((2, 6)), dma((2, 8)), dma((2, 8)), dma((16,)), dma((16,)),
            dma((3,)), dma((3,)), dma((19,)), dma((19,)),
        ],
        compiler_params=pltpu.CompilerParams(
            collective_id=0, has_side_effects=True, vmem_limit_bytes=32 * 2**20
        ),
        name="gather_and_relax",
    )(fixed_image[0], moving_patches[0], meta, prior_flow[0], mobility[0])
    ep = flow_call(gmeta, gi, gpl, gpr)
    net = pl.pallas_call(
        share_kernel,
        out_shape=sds((NP, SPAN, 128), f32),
        in_specs=[vmem_spec()],
        out_specs=any_spec(),
        scratch_shapes=[
            pltpu.VMEM((3, ROWS, 128), f32), pltpu.VMEM((ROWS, 128), f32),
            dma((3,)), dma((3,)), dma((19,)), dma((19,)), dma(()),
        ],
        compiler_params=pltpu.CompilerParams(collective_id=1, has_side_effects=True),
        name="share_flows",
    )(ep)
    flow, out = pl.pallas_call(
        settle_kernel,
        out_shape=(sds((2, PATCH_DEV), f32), sds((2, ROWS, COLS), f32)),
        in_specs=[vmem_spec()] * 3,
        out_specs=(vmem_spec(), vmem_spec()),
        scratch_shapes=[
            pltpu.VMEM((NP, 2, 1, HIGH, 128), f32),
            pltpu.VMEM((NP, 1, HIGH, 128), f32),
            pltpu.VMEM((NP, 2, 1, HIGH, 128), f32),
            pltpu.VMEM((NP, 2, 1, HIGH, 128), f32),
            pltpu.VMEM((NP, 2, 1, HIGH, 128), f32),
        ],
        compiler_params=pltpu.CompilerParams(vmem_limit_bytes=32 * 2**20),
        name="settle",
    )(net, mob_band, u_own)
    return flow[None], out[None]


def solution(mesh):
    in_specs = (
        P("pair", "tile", None),
        P("pair", "tile", None, None),
        P("pair", "tile"),
        P("pair", "tile", None),
        P("pair", "tile", None),
        P("pair", None, "tile", None),
    )
    out_specs = (P("pair", None, "tile"), P("pair", None, "tile", None))
    return jax.shard_map(shards, mesh=mesh, in_specs=in_specs, out_specs=out_specs, check_vma=False)
```

```python
import functools
import math

import jax
import jax.numpy as jnp
import ml_dtypes
import numpy as np
from jax import lax
from jax.experimental import pallas as pl
from jax.experimental.pallas import tpu as pltpu
from jax.sharding import PartitionSpec as P

MESH = pl.DeviceIdType.MESH
NY, NZ, NC, NP = 4, 8, 2, 4
TILES = NY * NZ * NC
W = 160
TILE = 512
PATCH_DEV = 32
STEPS = 32
EPS = 1e-06
ROWS = 16
COLS = 512
TILES_X = COLS // 128
HALO = 32
PAD = 8
SPAN = ROWS + 2 * HALO
HIGH = SPAN + 2 * PAD
HALF = W // 2 + 1
BLK = 88
FREQ = 2 * BLK
WIN_ROWS = 176
WIN_COLS = 384
GROUP = 8
DEPTH = 2


def device_at(y, z, c):
    return {"tile": (y * NZ + z) * NC + c}


def my_place():
    t = lax.axis_index("tile")
    return t, t // (NZ * NC), (t // NC) % NZ, t % NC


def halo_targets(t, p):
    for dp in range(NP):
        for d in range(-2, 3):
            if dp or d:
                there = {"tile": (t + d + TILES) % TILES, "pair": (p + dp) % NP}
                yield dp, d, there


def remote(src, dst, send, recv, device):
    return pltpu.make_async_remote_copy(
        src_ref=src, dst_ref=dst, send_sem=send, recv_sem=recv, device_id=device, device_id_type=MESH
    )


def greet(devices):
    barrier = pltpu.get_barrier_semaphore()
    for device in devices:
        pl.semaphore_signal(barrier, inc=1, device_id=device, device_id_type=MESH)
    pl.semaphore_wait(barrier, len(devices))


def relax_step(t, target, u_in, u_out, vel, mob, first, last, tiles):
    shape = (NP, tiles, 8, 128)
    lane = lax.broadcasted_iota(jnp.int32, shape, 3)
    line = lax.broadcasted_iota(jnp.int32, shape, 2)
    own = PAD + HALO
    for rows in range(first, last, 8):
        here = pl.ds(rows, 8)
        for comp in range(u_in.shape[1]):
            u = u_in[:, comp, :, here, :]
            above = u_in[:, comp, :, pl.ds(rows - 1, 8), :]
            below = u_in[:, comp, :, pl.ds(rows + 1, 8), :]
            if rows in (own, own - ROWS):
                above = jnp.where((line == 0) & (t == (own - rows) // ROWS), u, above)
            if rows + 8 in (own + ROWS, own + 2 * ROWS):
                below = jnp.where((line == 7) & (t == TILES - (rows + 8 - own) // ROWS), u, below)
            left, right = pltpu.roll(u, 1, axis=3), pltpu.roll(u, 127, axis=3)
            if tiles > 1:
                left = jnp.where(lane == 0, jnp.concatenate([u[:, :1], left[:, :-1]], axis=1), left)
                right = jnp.where(lane == 127, jnp.concatenate([right[:, 1:], u[:, -1:]], axis=1), right)
            inter = jnp.concatenate([u[:1], u[:-1]], axis=0) + jnp.concatenate([u[1:], u[-1:]], axis=0)
            force = ((above + below) + (left + right)) + (0.2 / 0.35) * inter
            force = force + target[:, comp, :, here, :] - (4.0 + 0.7 / 0.35) * u
            speed = 0.8 * vel[:, comp, :, here, :] + mob(here) * force
            vel[:, comp, :, here, :] = speed
            u_out[:, comp, :, here, :] = u + speed


def gather_kernel(
    img, pat, meta, prior_hbm, mob_hbm, gi, gpl, gpr, gmeta, u_own, mob_band,
    prior, mob, pv, pr, fine, own, net, target, mobs, ua, ub, vel, res, got,
    lsem, ysend, yrecv, zsend, zrecv, dsend, drecv, msend, mrecv, hsend, hrecv, rsend, rrecv,
):
    t, y, z, c = my_place()
    p = lax.axis_index("pair")
    right_y, left_y = device_at((y + 1) % NY, z, c), device_at((y + NY - 1) % NY, z, c)
    right_z, left_z = device_at(y, (z + 1) % NZ, c), device_at(y, (z + NZ - 1) % NZ, c)
    across_y = device_at((y + 2) % NY, z, c)
    sibling = device_at(y, z, 1 - c)
    stage = pltpu.make_async_copy(pat, pv, lsem.at[0])
    stage.start()
    strips = [
        pltpu.make_async_copy(prior_hbm, prior, lsem.at[2]),
        pltpu.make_async_copy(mob_hbm, mob, lsem.at[3]),
    ]
    for copy in strips:
        copy.start()
    mine = z * NC + c
    keep = pltpu.make_async_copy(img, gi.at[mine], lsem.at[1])
    keep.start()
    halo = list(halo_targets(t, p))
    greet([right_y, left_y, across_y, right_z, left_z, sibling] + [device for _, _, device in halo])

    lo, hi = pl.ds(0, 16), pl.ds(16, 16)
    glo, ghi = pl.ds(0, 4), pl.ds(4, 4)
    left_part = pl.ds(0, 128)
    sent = []
    yr, yl = [], []

    def start(copy, into=None):
        copy.start()
        sent.append(copy)
        if into is not None:
            into.append(copy)
        return copy

    def y_left(which, first, side, device, slot):
        return remote(
            pat.at[which, :, left_part], gpl.at[first, which], ysend.at[side, slot], yrecv.at[side, slot], device
        )

    start(y_left(hi, y, 0, right_y, 0), yr)
    start(y_left(lo, y, 1, left_y, 0), yl)

    half = TILE // 2
    zr, zl, dd = [], [], []
    for q in range(2):
        rs = pl.ds(q * half, half)
        start(remote(img.at[rs], gi.at[mine, rs], zsend.at[0, q], zrecv.at[0, q], right_z), zr)
        rs = pl.ds((1 - q) * half, half)
        start(remote(img.at[rs], gi.at[mine, rs], zsend.at[1, q], zrecv.at[1, q], left_z), zl)
    for copy in strips:
        copy.wait()
    for n in range(TILES_X):
        columns = pl.ds(128 * n, 128)
        fine[0:2, n] = prior[:, :, columns]
        fine[2, n] = mob[:, columns]
    for v in range(NP):
        own[v, 0:3] = fine[v % 2, v // 2 : v // 2 + 3].astype(jnp.bfloat16)
        own[v, 3:7] = fine[2].astype(jnp.bfloat16)
    meshes = []
    for n, (dp, d, device) in enumerate(halo):
        rows = pl.ds(ROWS * (2 - d), ROWS)
        copy = remote(own.at[(p + dp) % NP], net.at[p, :, rows, :], hsend.at[n], hrecv.at[n], device)
        start(copy, meshes)

    start(y_left(lo, y, 0, right_y, 1), yr)
    start(y_left(hi, y, 1, left_y, 1), yl)
    metas = []
    for n, device in enumerate((right_y, left_y, across_y)):
        start(remote(meta, gmeta.at[y], msend.at[n], mrecv.at[n], device), metas)
    start(remote(img, gi.at[mine], dsend.at[0], drecv.at[0], sibling), dd)

    stage.wait()
    for g in range(PATCH_DEV // 4):
        pr[g] = jnp.concatenate([pv[4 * g + q, :, 128:W] for q in range(4)], axis=1)
    pairs = []
    pairs.append(start(remote(pr.at[ghi], gpr.at[y, ghi], ysend.at[0, 3], yrecv.at[0, 3], right_y)))
    pairs.append(start(remote(pr.at[glo], gpr.at[y, glo], ysend.at[1, 3], yrecv.at[1, 3], left_y)))
    pairs.append(start(remote(pr.at[glo], gpr.at[y, glo], ysend.at[0, 4], yrecv.at[0, 4], right_y)))
    pairs.append(start(remote(pr.at[ghi], gpr.at[y, ghi], ysend.at[1, 4], yrecv.at[1, 4], left_y)))
    local = [
        pltpu.make_async_copy(pv.at[:, :, left_part], gpl.at[y], lsem.at[2]),
        pltpu.make_async_copy(pr, gpr.at[y], lsem.at[3]),
        pltpu.make_async_copy(meta, gmeta.at[y], lsem.at[4]),
    ]
    for copy in local:
        copy.start()

    def forward_z(k, q):
        for side, hops, device in ((0, NZ - k, right_z), (1, k, left_z)):
            slot = ((z + hops) % NZ) * NC + c
            part = q if side == 0 else 1 - q
            rs = pl.ds(part * half, half)
            line = zr if side == 0 else zl
            line[2 * (k - 1) + q].wait_recv()
            block = gi.at[slot, rs]
            if k < 3 or (k == 3 and q == 0):
                start(remote(block, block, zsend.at[side, 2 * k + q], zrecv.at[side, 2 * k + q], device), line)
            n = len(dd)
            start(remote(block, block, dsend.at[n], drecv.at[n], sibling), dd)

    middle = pl.ds(PAD + HALO, ROWS)
    comp, side = p % 2, p // 2

    def begin():
        for copy in meshes:
            copy.wait_recv()
        net[p, :, HALO : HALO + ROWS, :] = own[p]
        edge = jnp.zeros((NP, 1, 3, PAD, 128), jnp.float32)
        for ref in (ua, ub):
            ref[:, :, :, 0:PAD, :] = edge
            ref[:, :, :, HIGH - PAD :, :] = edge

        @pl.loop(0, NP)
        def _(s):
            for b in range(SPAN // ROWS):
                rows = pl.ds(PAD + ROWS * b, ROWS)
                values = net[s, :, ROWS * b : ROWS * b + ROWS, :].astype(jnp.float32)
                ua[s, 0, :, rows, :] = values[0:3]
                ub[s, 0, :, rows, :] = values[0:3]
                vel[s, 0, :, rows, :] = jnp.zeros_like(values[0:3])
                target[s, 0, :, rows, :] = (0.3 / 0.35) * values[0:3]
                mobs[s, :, rows, :] = 0.35 * values[3:7]

        values = fine[comp, pl.ds(side, 3)]
        ua[p, 0, :, middle, :] = values
        target[p, 0, :, middle, :] = (0.3 / 0.35) * values
        mobs[p, :, middle, :] = 0.35 * fine[2]

    def relax(first):
        @pl.loop(0, 4)
        def _(_):
            for u_in, u_out in ((ua, ub), (ub, ua)):
                relax_step(
                    t, target, u_in, u_out, vel, lambda here: mobs[:, pl.ds(side, 3), here, :],
                    PAD + first, HIGH - PAD - first, 3,
                )

    def forward_y():
        for copy in (yr[0], yl[0], pairs[0], pairs[1]):
            copy.wait_recv()
        before, after = (y + NY - 1) % NY, (y + 1) % NY
        for side, first, which, groups, device in ((0, before, hi, ghi, right_y), (1, after, lo, glo, left_y)):
            block = gpl.at[first, which]
            start(remote(block, block, ysend.at[side, 2], yrecv.at[side, 2], device), far)
            block = gpr.at[first, groups]
            start(remote(block, block, ysend.at[side, 5], yrecv.at[side, 5], device), far)

    far = []
    forward_z(1, 0)
    forward_z(1, 1)
    forward_z(2, 0)
    forward_y()
    begin()
    relax(0)
    forward_z(2, 1)
    relax(8)
    forward_z(3, 0)
    relax(16)
    forward_z(3, 1)
    relax(24)
    res[...] = ua[:, 0, pl.ds(side, 2), middle, :]
    results = []
    for d in range(1, NP):
        to = (p + d) % NP
        start(remote(res.at[to], got.at[p], rsend.at[d - 1], rrecv.at[d - 1], {"pair": to}), results)
    got[p] = res[p]
    forward_z(4, 0)
    for copy in results:
        copy.wait_recv()
    for v in range(NP):
        for n in range(2):
            first = 128 * (v // 2 * 2 + n)
            u_own[v % 2, :, first : first + 128] = got[v, n]
    lane = lax.broadcasted_iota(jnp.int32, (SPAN, 128), 1)
    for s in range(NP):
        parts = [mobs[s, n, PAD : PAD + SPAN, :] for n in range(4)]
        low = jnp.where(lane < 32, pltpu.roll(parts[0], 32, axis=1), pltpu.roll(parts[1], 32, axis=1))
        top = jnp.where(lane < 96, pltpu.roll(parts[2], 96, axis=1), pltpu.roll(parts[3], 96, axis=1))
        mob_band[s] = jnp.where(lane < 64, low, top)

    for copy in yr[1:] + yl[1:] + pairs[2:] + far + metas + dd:
        copy.wait_recv()
    for copy in sent:
        copy.wait_send()
    for copy in local:
        copy.wait()
    keep.wait()


def flow_kernel(
    meta, gi, gpl, gpr, rows_hbm, cols_hbm, left_hbm, right_hbm, out,
    items, rows_tab, cols_tab, inv_left, inv_right, xbuf, mbuf, lines, halves, backs, sum_e, sum_r, sems, tsems,
):
    _, y, _, _ = my_place()
    tables = [
        pltpu.make_async_copy(src, dst, tsems.at[n])
        for n, (src, dst) in enumerate(
            ((cols_hbm, cols_tab), (rows_hbm, rows_tab), (left_hbm, inv_left), (right_hbm, inv_right))
        )
    ]

    for copy in tables:
        copy.start()

    def note(h, count):
        for j in range(PATCH_DEV):
            items[count] = h * PATCH_DEV + j
            count = count + (meta[h, 0, j] // (NZ * NC) == y).astype(jnp.int32)
        return count

    count = lax.fori_loop(0, NY, note, jnp.int32(0))
    sum_e[...] = jnp.zeros_like(sum_e)
    sum_r[...] = jnp.zeros_like(sum_r)
    rounds = (count + GROUP - 1) // GROUP

    def item(step, g):
        n = items[jnp.minimum(step * GROUP + g, count - 1)]
        return n // PATCH_DEV, n % PATCH_DEV

    def place(h, j):
        first_row, first_col = meta[h, 1, j], meta[h, 2, j]
        row = jnp.minimum(first_row // 16 * 16, TILE - WIN_ROWS)
        col = first_col // 128 * 128
        return row, first_row - row, col, first_col - col

    def copies(step, slot, g):
        h, j = item(step, g)
        row, _, col, _ = place(h, j)
        image = gi.at[meta[h, 0, j] % (NZ * NC)]
        rows = pl.ds(pl.multiple_of(row, 16), WIN_ROWS)
        third = jnp.minimum(col + 256, TILE - 128)
        pieces = (
            (image.at[rows, pl.ds(pl.multiple_of(col, 128), 256)], xbuf.at[slot, g, :, pl.ds(0, 256)]),
            (image.at[rows, pl.ds(pl.multiple_of(third, 128), 128)], xbuf.at[slot, g, :, pl.ds(256, 128)]),
            (gpl.at[h, j], mbuf.at[slot, g, :, pl.ds(0, 128)]),
            (gpr.at[h, j // 4], mbuf.at[slot, g, :, pl.ds(128, 128)]),
        )
        return [pltpu.make_async_copy(src, dst, sems.at[slot, g, n]) for n, (src, dst) in enumerate(pieces)]

    def fetch(step, slot):
        for g in range(GROUP):
            for copy in copies(step, slot, g):
                copy.start()

    def dot(a, b):
        return jnp.dot(a, b, preferred_element_type=jnp.float32)

    signed = lax.broadcasted_iota(jnp.int32, (W, 256), 0)
    signed = jnp.where(signed < W // 2, signed, signed - W).astype(jnp.float32)
    win_lane = lax.broadcasted_iota(jnp.int32, (WIN_ROWS, 128), 1)
    base = GROUP * WIN_ROWS

    def turn(x, amount):
        return pltpu.roll(x.astype(jnp.float32), (128 - amount) % 128, axis=1)

    def work(step, slot):
        place_of = []
        for g in range(GROUP):
            h, j = item(step, g)
            _, row_shift, _, col_shift = place(h, j)
            place_of.append((h, j, row_shift))
            parts = [turn(xbuf[slot, g, :, 128 * n : 128 * n + 128], col_shift) for n in range(3)]
            inside = win_lane < 128 - col_shift
            rows = pl.ds(g * WIN_ROWS, WIN_ROWS)
            lines[rows, 0:128] = jnp.where(inside, parts[0], parts[1]).astype(jnp.bfloat16)
            lines[rows, 128:256] = jnp.where(inside, parts[1], parts[2]).astype(jnp.bfloat16)
            rows = pl.ds(base + g * W, W)
            lines[rows, 0:128] = mbuf[slot, g, :, 0:128]
            lines[rows, 128:256] = turn(mbuf[slot, g, :, 128:256], j % 4 * 32).astype(jnp.bfloat16)
        halves[...] = dot(lines[...], cols_tab[...]).astype(jnp.bfloat16)
        spectra = [
            (
                dot(rows_tab[place_of[g][2]], halves[pl.ds(g * WIN_ROWS, WIN_ROWS), :]),
                dot(rows_tab[0, :, 0:W], halves[pl.ds(base + g * W, W), :]),
            )
            for g in range(GROUP)
        ]
        crosses = []
        for g in range(GROUP):
            fixed, moving = spectra[g]
            fcc, fcs, fsc, fss = fixed[:BLK, :128], fixed[:BLK, 128:], fixed[BLK:, :128], fixed[BLK:, 128:]
            mcc, mcs, msc, mss = moving[:BLK, :128], moving[:BLK, 128:], moving[BLK:, :128], moving[BLK:, 128:]
            ee = fcc * mcc + fss * mss + fcs * mcs + fsc * msc
            oo = fcc * mss + fss * mcc - fcs * msc - fsc * mcs
            eo = fcc * mcs - fcs * mcc + fsc * mss - fss * msc
            oe = fcc * msc - fsc * mcc + fcs * mss - fss * mcs
            cross = jnp.concatenate(
                [jnp.concatenate([ee, eo], axis=1), jnp.concatenate([oe, oo], axis=1)], axis=0
            ).astype(jnp.bfloat16)
            crosses.append(cross)
        for g in range(GROUP):
            backs[pl.ds(g * W, W), :] = dot(inv_left[...], crosses[g]).astype(jnp.bfloat16)
        corr = dot(backs[...], inv_right[...])
        for g in range(GROUP):
            h, j, _ = place_of[g]
            energy = corr[g * W : g * W + W]
            energy = energy * energy
            at = pl.ds(h * PATCH_DEV + j % 2 * ROWS + j // 2, 1)
            sum_e[at, :] = jnp.sum(energy, axis=0, keepdims=True)
            sum_r[at, :] = jnp.sum(energy * signed, axis=0, keepdims=True)

    @pl.when(rounds > 0)
    def _():
        fetch(0, 0)

    def one(step, carry):
        slot = step % DEPTH

        @pl.when(step + 1 < rounds)
        def _():
            fetch(step + 1, (step + 1) % DEPTH)

        for g in range(GROUP):
            for copy in copies(step, slot, g):
                copy.wait()
        work(step, slot)
        return carry

    for copy in tables:
        copy.wait()
    lax.fori_loop(0, rounds, one, 0)

    number = lax.broadcasted_iota(jnp.int32, (NY * PATCH_DEV, 256), 1)
    shift = jnp.where(number < W // 2, number, number - W).astype(jnp.float32)
    plain = sum_e[...]
    total = jnp.sum(plain, axis=1, keepdims=True) + EPS
    flows = (
        jnp.sum(sum_r[...], axis=1, keepdims=True) / total,
        jnp.sum(plain * shift, axis=1, keepdims=True) / total,
    )
    lane = lax.broadcasted_iota(jnp.int32, (ROWS, 128), 1)
    for h in range(NY):
        block = jnp.zeros((ROWS, 128), jnp.float32)
        for comp in range(2):
            for side in range(2):
                first = h * PATCH_DEV + side * ROWS
                block = jnp.where(lane == 32 + 64 * side + comp, flows[comp][first : first + ROWS], block)
        out[h] = block


def share_kernel(ep, net, got, total, fsend, frecv, hsend, hrecv, lsem):
    t, y, z, c = my_place()
    p = lax.axis_index("pair")
    homes = [device_at((y + d) % NY, z, c) for d in range(1, NY)]
    halo = list(halo_targets(t, p))
    greet(homes + [device for _, _, device in halo])
    first = []
    for n, device in enumerate(homes):
        copy = remote(ep.at[(y + n + 1) % NY], got.at[n], fsend.at[n], frecv.at[n], device)
        copy.start()
        first.append(copy)
    for copy in first:
        copy.wait_recv()
    total[...] = ep[y] + got[0] + got[1] + got[2]
    second = []
    for n, (dp, d, device) in enumerate(halo):
        copy = remote(total, net.at[p, pl.ds(ROWS * (2 - d), ROWS), :], hsend.at[n], hrecv.at[n], device)
        copy.start()
        second.append(copy)
    own = pltpu.make_async_copy(total, net.at[p, pl.ds(HALO, ROWS), :], lsem)
    own.start()
    for copy in second:
        copy.wait_recv()
    for copy in first + second:
        copy.wait_send()
    own.wait()


def settle_kernel(net, mob_band, u_own, flow, out, tgt, mob, ua, ub, vel):
    t = lax.axis_index("tile")
    p = lax.axis_index("pair")
    lane = lax.broadcasted_iota(jnp.int32, (SPAN, 128), 1)
    node = (lane == 32) | (lane == 96)
    span = pl.ds(PAD, SPAN)
    vel[...] = jnp.zeros_like(vel)
    ua[...] = jnp.zeros_like(ua)
    ub[...] = jnp.zeros_like(ub)
    for s in range(NP):
        values = net[s]
        for comp in range(2):
            turned = values if comp == 0 else pltpu.roll(values, 127, axis=1)
            tgt[s, comp, 0, span, :] = (0.3 / 0.35) * jnp.where(node, turned, 0.0)
        mob[s, 0, span, :] = mob_band[s]

    for first in range(0, STEPS, 8):

        @pl.loop(0, 4)
        def _(_):
            for u_in, u_out in ((ua, ub), (ub, ua)):
                relax_step(
                    t, tgt, u_in, u_out, vel, lambda here: mob[:, :, here, :], PAD + first, HIGH - PAD - first, 1
                )

    middle = pl.ds(PAD + HALO, ROWS)
    lane = lax.broadcasted_iota(jnp.int32, (ROWS, 128), 1)
    row = lax.broadcasted_iota(jnp.int32, (ROWS, 128), 0)
    for comp in range(2):
        moved = jnp.zeros((ROWS, 128), jnp.float32)
        given = net[p, HALO : HALO + ROWS, :]
        for s in range(NP):
            moved = jnp.where(p == s, ua[s, comp, 0, middle, :], moved)
        wide, narrow = pltpu.roll(moved, 96, axis=1), pltpu.roll(moved, 32, axis=1)
        for n, (part, inside) in enumerate(((wide, lane >= 96), (wide, lane < 32), (narrow, lane >= 96), (narrow, lane < 32))):
            columns = pl.ds(128 * n, 128)
            out[comp, :, columns] = u_own[comp, :, columns] + jnp.where(inside, part, 0.0)
        even = jnp.sum(jnp.where(lane == 32 + comp, given, 0.0), axis=1, keepdims=True)
        odd = jnp.sum(jnp.where(lane == 96 + comp, given, 0.0), axis=1, keepdims=True)
        spread = jnp.where(lane == 2 * row, even, 0.0) + jnp.where(lane == 2 * row + 1, odd, 0.0)
        flow[comp : comp + 1, :] = jnp.sum(spread, axis=0, keepdims=True)[:, :PATCH_DEV]


def make_tables():
    numbers = np.arange(W)
    phase = (numbers[:, None] * numbers[None, :] % W).astype(np.float32) * np.float32(2.0 * math.pi / W)
    scale = np.float32(1.0 / math.sqrt(W))
    cos = (np.cos(phase) * scale).astype(ml_dtypes.bfloat16).astype(np.float32)
    sin = (np.sin(phase) * scale).astype(ml_dtypes.bfloat16).astype(np.float32)
    left = np.zeros((FREQ, W), np.float32)
    left[:HALF], left[BLK : BLK + HALF] = cos[:HALF], sin[:HALF]
    right = np.zeros((W, 256), np.float32)
    right[:, :HALF], right[:, 128 : 128 + HALF] = cos[:, :HALF], sin[:, :HALF]
    rows_tab = np.zeros((17, FREQ, WIN_ROWS), np.float32)
    for shift in range(17):
        rows_tab[shift, :, shift : shift + W] = left
    cols_tab = np.zeros((256, 256), np.float32)
    cols_tab[:W] = right
    weight = np.full((HALF, 1), 2.0, np.float32)
    weight[0] = weight[-1] = 1.0
    inv_left = np.zeros((W, FREQ), np.float32)
    inv_left[:, :HALF], inv_left[:, BLK : BLK + HALF] = (weight * cos[:HALF]).T, (-2.0 * sin[:HALF]).T
    inv_right = np.zeros((256, 256), np.float32)
    inv_right[:HALF, :W], inv_right[128 : 128 + HALF, :W] = weight * cos[:HALF], -2.0 * sin[:HALF]
    half = lambda table: table.astype(ml_dtypes.bfloat16)
    return half(rows_tab), half(cols_tab), half(inv_left), half(inv_right)


def any_spec():
    return pl.BlockSpec(memory_space=pl.ANY)


def hbm_spec():
    return pl.BlockSpec(memory_space=pltpu.HBM)


def vmem_spec():
    return pl.BlockSpec(memory_space=pltpu.VMEM)


def flow_call(gmeta, gi, gpl, gpr):
    f32, bf16 = jnp.float32, jnp.bfloat16
    tables = [jnp.asarray(table) for table in make_tables()]
    return pl.pallas_call(
        flow_kernel,
        out_shape=jax.ShapeDtypeStruct((NY, ROWS, 128), f32),
        in_specs=[pl.BlockSpec(memory_space=pltpu.SMEM)] + [any_spec()] * 3 + [hbm_spec()] * 4,
        out_specs=vmem_spec(),
        scratch_shapes=[
            pltpu.SMEM((NY * PATCH_DEV + 1,), jnp.int32),
            pltpu.VMEM((17, FREQ, WIN_ROWS), bf16),
            pltpu.VMEM((256, 256), bf16),
            pltpu.VMEM((W, FREQ), bf16),
            pltpu.VMEM((256, 256), bf16),
            pltpu.VMEM((DEPTH, GROUP, WIN_ROWS, WIN_COLS), bf16),
            pltpu.VMEM((DEPTH, GROUP, W, 256), bf16),
            pltpu.VMEM((GROUP * (WIN_ROWS + W), 256), bf16),
            pltpu.VMEM((GROUP * (WIN_ROWS + W), 256), bf16),
            pltpu.VMEM((GROUP * W, 256), bf16),
            pltpu.VMEM((NY * PATCH_DEV, 256), f32),
            pltpu.VMEM((NY * PATCH_DEV, 256), f32),
            pltpu.SemaphoreType.DMA((DEPTH, GROUP, 4)),
            pltpu.SemaphoreType.DMA((4,)),
        ],
        compiler_params=pltpu.CompilerParams(vmem_limit_bytes=60 * 2**20),
        name="patch_flows",
    )(gmeta, gi, gpl, gpr, *tables)


def shards(fixed_image, moving_patches, owners, offsets, mobility, prior_flow):
    meta = jnp.pad(jnp.concatenate([owners, offsets[0].T], axis=0), ((0, 5), (0, 96)))
    f32, bf16 = jnp.float32, jnp.bfloat16
    sds = jax.ShapeDtypeStruct
    dma = pltpu.SemaphoreType.DMA
    gi, gpl, gpr, gmeta, u_own, mob_band = pl.pallas_call(
        gather_kernel,
        out_shape=(
            sds((NZ * NC, TILE, TILE), bf16),
            sds((NY, PATCH_DEV, W, 128), bf16),
            sds((NY, PATCH_DEV // 4, W, 128), bf16),
            sds((NY, 8, 128), jnp.int32),
            sds((2, ROWS, COLS), f32),
            sds((NP, SPAN, 128), f32),
        ),
        in_specs=[hbm_spec(), hbm_spec(), vmem_spec(), hbm_spec(), hbm_spec()],
        out_specs=(any_spec(), any_spec(), any_spec(), any_spec(), vmem_spec(), vmem_spec()),
        scratch_shapes=[
            pltpu.VMEM((2, ROWS, COLS), f32),
            pltpu.VMEM((ROWS, COLS), f32),
            pltpu.VMEM((PATCH_DEV, W, W), bf16),
            pltpu.VMEM((PATCH_DEV // 4, W, 128), bf16),
            pltpu.VMEM((3, TILES_X, ROWS, 128), f32),
            pltpu.VMEM((NP, 7, ROWS, 128), bf16),
            pltpu.VMEM((NP, 7, SPAN, 128), bf16),
            pltpu.VMEM((NP, 1, 3, HIGH, 128), f32),
            pltpu.VMEM((NP, TILES_X, HIGH, 128), f32),
            pltpu.VMEM((NP, 1, 3, HIGH, 128), f32),
            pltpu.VMEM((NP, 1, 3, HIGH, 128), f32),
            pltpu.VMEM((NP, 1, 3, HIGH, 128), f32),
            pltpu.VMEM((NP, 2, ROWS, 128), f32),
            pltpu.VMEM((NP, 2, ROWS, 128), f32),
            dma((5,)), dma((2, 6)), dma((2, 6)), dma((2, 8)), dma((2, 8)), dma((16,)), dma((16,)),
            dma((3,)), dma((3,)), dma((19,)), dma((19,)), dma((3,)), dma((3,)),
        ],
        compiler_params=pltpu.CompilerParams(
            collective_id=0, has_side_effects=True, vmem_limit_bytes=60 * 2**20
        ),
        name="gather_and_relax",
    )(fixed_image[0], moving_patches[0], meta, prior_flow[0], mobility[0])
    ep = flow_call(gmeta, gi, gpl, gpr)
    net = pl.pallas_call(
        share_kernel,
        out_shape=sds((NP, SPAN, 128), f32),
        in_specs=[vmem_spec()],
        out_specs=any_spec(),
        scratch_shapes=[
            pltpu.VMEM((3, ROWS, 128), f32), pltpu.VMEM((ROWS, 128), f32),
            dma((3,)), dma((3,)), dma((19,)), dma((19,)), dma(()),
        ],
        compiler_params=pltpu.CompilerParams(collective_id=1, has_side_effects=True),
        name="share_flows",
    )(ep)
    flow, out = pl.pallas_call(
        settle_kernel,
        out_shape=(sds((2, PATCH_DEV), f32), sds((2, ROWS, COLS), f32)),
        in_specs=[vmem_spec()] * 3,
        out_specs=(vmem_spec(), vmem_spec()),
        scratch_shapes=[
            pltpu.VMEM((NP, 2, 1, HIGH, 128), f32),
            pltpu.VMEM((NP, 1, HIGH, 128), f32),
            pltpu.VMEM((NP, 2, 1, HIGH, 128), f32),
            pltpu.VMEM((NP, 2, 1, HIGH, 128), f32),
            pltpu.VMEM((NP, 2, 1, HIGH, 128), f32),
        ],
        compiler_params=pltpu.CompilerParams(vmem_limit_bytes=60 * 2**20),
        name="settle",
    )(net, mob_band, u_own)
    return flow[None], out[None]


def solution(mesh):
    in_specs = (
        P("pair", "tile", None),
        P("pair", "tile", None, None),
        P("pair", "tile"),
        P("pair", "tile", None),
        P("pair", "tile", None),
        P("pair", None, "tile", None),
    )
    out_specs = (P("pair", None, "tile"), P("pair", None, "tile", None))
    return jax.shard_map(shards, mesh=mesh, in_specs=in_specs, out_specs=out_specs, check_vma=False)
```

```python
import functools
import math

import jax
import jax.numpy as jnp
import ml_dtypes
import numpy as np
from jax import lax
from jax.experimental import pallas as pl
from jax.experimental.pallas import tpu as pltpu
from jax.sharding import PartitionSpec as P

MESH = pl.DeviceIdType.MESH
NY, NZ, NC, NP = 4, 8, 2, 4
TILES = NY * NZ * NC
W = 160
TILE = 512
PATCH_DEV = 32
STEPS = 32
EPS = 1e-06
ROWS = 16
COLS = 512
TILES_X = COLS // 128
HALO = 32
PAD = 8
SPAN = ROWS + 2 * HALO
HIGH = SPAN + 2 * PAD
HALF = W // 2 + 1
BLK = 88
FREQ = 2 * BLK
WIN_ROWS = 176
WIN_COLS = 384
GROUP = 8
DEPTH = 2


def device_at(y, z, c):
    return {"tile": (y * NZ + z) * NC + c}


def my_place():
    t = lax.axis_index("tile")
    return t, t // (NZ * NC), (t // NC) % NZ, t % NC


def halo_targets(t, p):
    for dp in range(NP):
        for d in range(-2, 3):
            if dp or d:
                there = {"tile": (t + d + TILES) % TILES, "pair": (p + dp) % NP}
                yield dp, d, there


def remote(src, dst, send, recv, device):
    return pltpu.make_async_remote_copy(
        src_ref=src, dst_ref=dst, send_sem=send, recv_sem=recv, device_id=device, device_id_type=MESH
    )


def greet(devices):
    barrier = pltpu.get_barrier_semaphore()
    for device in devices:
        pl.semaphore_signal(barrier, inc=1, device_id=device, device_id_type=MESH)
    pl.semaphore_wait(barrier, len(devices))


def relax_step(t, target, u_in, u_out, vel, mob, first, last, tiles):
    shape = (NP, tiles, 8, 128)
    lane = lax.broadcasted_iota(jnp.int32, shape, 3)
    line = lax.broadcasted_iota(jnp.int32, shape, 2)
    own = PAD + HALO
    for rows in range(first, last, 8):
        here = pl.ds(rows, 8)
        for comp in range(u_in.shape[1]):
            u = u_in[:, comp, :, here, :]
            above = u_in[:, comp, :, pl.ds(rows - 1, 8), :]
            below = u_in[:, comp, :, pl.ds(rows + 1, 8), :]
            if rows in (own, own - ROWS):
                above = jnp.where((line == 0) & (t == (own - rows) // ROWS), u, above)
            if rows + 8 in (own + ROWS, own + 2 * ROWS):
                below = jnp.where((line == 7) & (t == TILES - (rows + 8 - own) // ROWS), u, below)
            left, right = pltpu.roll(u, 1, axis=3), pltpu.roll(u, 127, axis=3)
            if tiles > 1:
                left = jnp.where(lane == 0, jnp.concatenate([u[:, :1], left[:, :-1]], axis=1), left)
                right = jnp.where(lane == 127, jnp.concatenate([right[:, 1:], u[:, -1:]], axis=1), right)
            inter = jnp.concatenate([u[:1], u[:-1]], axis=0) + jnp.concatenate([u[1:], u[-1:]], axis=0)
            force = ((above + below) + (left + right)) + (0.2 / 0.35) * inter
            force = force + target[:, comp, :, here, :] - (4.0 + 0.7 / 0.35) * u
            speed = 0.8 * vel[:, comp, :, here, :] + mob(here) * force
            vel[:, comp, :, here, :] = speed
            u_out[:, comp, :, here, :] = u + speed


def gather_kernel(
    img, pat, owners, offsets, prior_hbm, mob_hbm, gi, gpl, gpr, gmeta, u_own, mob_band,
    meta, own_v, off_v, prior, mob, pv, pr, fine, own, net, target, mobs, ua, ub, vel, res, got,
    lsem, ysend, yrecv, zsend, zrecv, dsend, drecv, msend, mrecv, hsend, hrecv, rsend, rrecv,
):
    t, y, z, c = my_place()
    p = lax.axis_index("pair")
    right_y, left_y = device_at((y + 1) % NY, z, c), device_at((y + NY - 1) % NY, z, c)
    right_z, left_z = device_at(y, (z + 1) % NZ, c), device_at(y, (z + NZ - 1) % NZ, c)
    across_y = device_at((y + 2) % NY, z, c)
    sibling = device_at(y, z, 1 - c)
    stage = pltpu.make_async_copy(pat, pv, lsem.at[0])
    stage.start()
    strips = [
        pltpu.make_async_copy(prior_hbm, prior, lsem.at[2]),
        pltpu.make_async_copy(mob_hbm, mob, lsem.at[3]),
        pltpu.make_async_copy(owners, own_v, lsem.at[4]),
        pltpu.make_async_copy(offsets, off_v, lsem.at[5]),
    ]
    for copy in strips:
        copy.start()
    mine = z * NC + c
    keep = pltpu.make_async_copy(img, gi.at[mine], lsem.at[1])
    keep.start()
    halo = list(halo_targets(t, p))
    greet([right_y, left_y, across_y, right_z, left_z, sibling] + [device for _, _, device in halo])

    lo, hi = pl.ds(0, 16), pl.ds(16, 16)
    glo, ghi = pl.ds(0, 4), pl.ds(4, 4)
    left_part = pl.ds(0, 128)
    sent = []
    yr, yl = [], []

    def start(copy, into=None):
        copy.start()
        sent.append(copy)
        if into is not None:
            into.append(copy)
        return copy

    def y_left(which, first, side, device, slot):
        return remote(
            pat.at[which, :, left_part], gpl.at[first, which], ysend.at[side, slot], yrecv.at[side, slot], device
        )

    start(y_left(hi, y, 0, right_y, 0), yr)
    start(y_left(lo, y, 1, left_y, 0), yl)

    half = TILE // 2
    zr, zl, dd = [], [], []
    for q in range(2):
        rs = pl.ds(q * half, half)
        start(remote(img.at[rs], gi.at[mine, rs], zsend.at[0, q], zrecv.at[0, q], right_z), zr)
        rs = pl.ds((1 - q) * half, half)
        start(remote(img.at[rs], gi.at[mine, rs], zsend.at[1, q], zrecv.at[1, q], left_z), zl)
    for copy in strips:
        copy.wait()
    meta[0:1, 0:PATCH_DEV] = own_v[...]
    meta[1:3, 0:PATCH_DEV] = off_v[...]
    for n in range(TILES_X):
        columns = pl.ds(128 * n, 128)
        fine[0:2, n] = prior[:, :, columns]
        fine[2, n] = mob[:, columns]
    for v in range(NP):
        own[v, 0:3] = fine[v % 2, v // 2 : v // 2 + 3].astype(jnp.bfloat16)
        own[v, 3:7] = fine[2].astype(jnp.bfloat16)
    meshes = []
    for n, (dp, d, device) in enumerate(halo):
        rows = pl.ds(ROWS * (2 - d), ROWS)
        copy = remote(own.at[(p + dp) % NP], net.at[p, :, rows, :], hsend.at[n], hrecv.at[n], device)
        start(copy, meshes)

    start(y_left(lo, y, 0, right_y, 1), yr)
    start(y_left(hi, y, 1, left_y, 1), yl)
    metas = []
    for n, device in enumerate((right_y, left_y, across_y)):
        start(remote(meta, gmeta.at[y], msend.at[n], mrecv.at[n], device), metas)
    start(remote(img, gi.at[mine], dsend.at[0], drecv.at[0], sibling), dd)

    stage.wait()
    for g in range(PATCH_DEV // 4):
        pr[g] = jnp.concatenate([pv[4 * g + q, :, 128:W] for q in range(4)], axis=1)
    pairs = []
    pairs.append(start(remote(pr.at[ghi], gpr.at[y, ghi], ysend.at[0, 3], yrecv.at[0, 3], right_y)))
    pairs.append(start(remote(pr.at[glo], gpr.at[y, glo], ysend.at[1, 3], yrecv.at[1, 3], left_y)))
    pairs.append(start(remote(pr.at[glo], gpr.at[y, glo], ysend.at[0, 4], yrecv.at[0, 4], right_y)))
    pairs.append(start(remote(pr.at[ghi], gpr.at[y, ghi], ysend.at[1, 4], yrecv.at[1, 4], left_y)))
    local = [
        pltpu.make_async_copy(pv.at[:, :, left_part], gpl.at[y], lsem.at[2]),
        pltpu.make_async_copy(pr, gpr.at[y], lsem.at[3]),
        pltpu.make_async_copy(meta, gmeta.at[y], lsem.at[4]),
    ]
    for copy in local:
        copy.start()

    def forward_z(k, q):
        for side, hops, device in ((0, NZ - k, right_z), (1, k, left_z)):
            slot = ((z + hops) % NZ) * NC + c
            part = q if side == 0 else 1 - q
            rs = pl.ds(part * half, half)
            line = zr if side == 0 else zl
            line[2 * (k - 1) + q].wait_recv()
            block = gi.at[slot, rs]
            if k < 3 or (k == 3 and q == 0):
                start(remote(block, block, zsend.at[side, 2 * k + q], zrecv.at[side, 2 * k + q], device), line)
            n = len(dd)
            start(remote(block, block, dsend.at[n], drecv.at[n], sibling), dd)

    middle = pl.ds(PAD + HALO, ROWS)
    comp, side = p % 2, p // 2

    def begin():
        for copy in meshes:
            copy.wait_recv()
        net[p, :, HALO : HALO + ROWS, :] = own[p]
        edge = jnp.zeros((NP, 1, 3, PAD, 128), jnp.float32)
        for ref in (ua, ub):
            ref[:, :, :, 0:PAD, :] = edge
            ref[:, :, :, HIGH - PAD :, :] = edge

        @pl.loop(0, NP)
        def _(s):
            for b in range(SPAN // ROWS):
                rows = pl.ds(PAD + ROWS * b, ROWS)
                values = net[s, :, ROWS * b : ROWS * b + ROWS, :].astype(jnp.float32)
                ua[s, 0, :, rows, :] = values[0:3]
                ub[s, 0, :, rows, :] = values[0:3]
                vel[s, 0, :, rows, :] = jnp.zeros_like(values[0:3])
                target[s, 0, :, rows, :] = (0.3 / 0.35) * values[0:3]
                mobs[s, :, rows, :] = 0.35 * values[3:7]

        values = fine[comp, pl.ds(side, 3)]
        ua[p, 0, :, middle, :] = values
        target[p, 0, :, middle, :] = (0.3 / 0.35) * values
        mobs[p, :, middle, :] = 0.35 * fine[2]

    def relax(first):
        @pl.loop(0, 4)
        def _(_):
            for u_in, u_out in ((ua, ub), (ub, ua)):
                relax_step(
                    t, target, u_in, u_out, vel, lambda here: mobs[:, pl.ds(side, 3), here, :],
                    PAD + first, HIGH - PAD - first, 3,
                )

    def forward_y():
        for copy in (yr[0], yl[0], pairs[0], pairs[1]):
            copy.wait_recv()
        before, after = (y + NY - 1) % NY, (y + 1) % NY
        for side, first, which, groups, device in ((0, before, hi, ghi, right_y), (1, after, lo, glo, left_y)):
            block = gpl.at[first, which]
            start(remote(block, block, ysend.at[side, 2], yrecv.at[side, 2], device), far)
            block = gpr.at[first, groups]
            start(remote(block, block, ysend.at[side, 5], yrecv.at[side, 5], device), far)

    far = []
    forward_z(1, 0)
    forward_z(1, 1)
    forward_z(2, 0)
    forward_y()
    begin()
    relax(0)
    forward_z(2, 1)
    relax(8)
    forward_z(3, 0)
    relax(16)
    forward_z(3, 1)
    relax(24)
    res[...] = ua[:, 0, pl.ds(side, 2), middle, :]
    results = []
    for d in range(1, NP):
        to = (p + d) % NP
        start(remote(res.at[to], got.at[p], rsend.at[d - 1], rrecv.at[d - 1], {"pair": to}), results)
    got[p] = res[p]
    forward_z(4, 0)
    for copy in results:
        copy.wait_recv()
    for v in range(NP):
        for n in range(2):
            first = 128 * (v // 2 * 2 + n)
            u_own[v % 2, :, first : first + 128] = got[v, n]
    lane = lax.broadcasted_iota(jnp.int32, (SPAN, 128), 1)
    for s in range(NP):
        parts = [mobs[s, n, PAD : PAD + SPAN, :] for n in range(4)]
        low = jnp.where(lane < 32, pltpu.roll(parts[0], 32, axis=1), pltpu.roll(parts[1], 32, axis=1))
        top = jnp.where(lane < 96, pltpu.roll(parts[2], 96, axis=1), pltpu.roll(parts[3], 96, axis=1))
        mob_band[s] = jnp.where(lane < 64, low, top)

    for copy in yr[1:] + yl[1:] + pairs[2:] + far + metas + dd:
        copy.wait_recv()
    for copy in sent:
        copy.wait_send()
    for copy in local:
        copy.wait()
    keep.wait()


def flow_kernel(
    meta, gi, gpl, gpr, rows_hbm, cols_hbm, left_hbm, right_hbm, out,
    items, rows_tab, cols_tab, inv_left, inv_right, xbuf, mbuf, lines, halves, backs, sum_e, sum_r, sems, tsems,
):
    _, y, _, _ = my_place()
    tables = [
        pltpu.make_async_copy(src, dst, tsems.at[n])
        for n, (src, dst) in enumerate(
            ((cols_hbm, cols_tab), (rows_hbm, rows_tab), (left_hbm, inv_left), (right_hbm, inv_right))
        )
    ]

    for copy in tables:
        copy.start()

    def note(h, count):
        for j in range(PATCH_DEV):
            items[count] = h * PATCH_DEV + j
            count = count + (meta[h, 0, j] // (NZ * NC) == y).astype(jnp.int32)
        return count

    count = lax.fori_loop(0, NY, note, jnp.int32(0))
    sum_e[...] = jnp.zeros_like(sum_e)
    sum_r[...] = jnp.zeros_like(sum_r)
    rounds = (count + GROUP - 1) // GROUP

    def item(step, g):
        n = items[jnp.minimum(step * GROUP + g, count - 1)]
        return n // PATCH_DEV, n % PATCH_DEV

    def place(h, j):
        first_row, first_col = meta[h, 1, j], meta[h, 2, j]
        row = jnp.minimum(first_row // 16 * 16, TILE - WIN_ROWS)
        col = first_col // 128 * 128
        return row, first_row - row, col, first_col - col

    def copies(step, slot, g):
        h, j = item(step, g)
        row, _, col, _ = place(h, j)
        image = gi.at[meta[h, 0, j] % (NZ * NC)]
        rows = pl.ds(pl.multiple_of(row, 16), WIN_ROWS)
        third = jnp.minimum(col + 256, TILE - 128)
        pieces = (
            (image.at[rows, pl.ds(pl.multiple_of(col, 128), 256)], xbuf.at[slot, g, :, pl.ds(0, 256)]),
            (image.at[rows, pl.ds(pl.multiple_of(third, 128), 128)], xbuf.at[slot, g, :, pl.ds(256, 128)]),
            (gpl.at[h, j], mbuf.at[slot, g, :, pl.ds(0, 128)]),
            (gpr.at[h, j // 4], mbuf.at[slot, g, :, pl.ds(128, 128)]),
        )
        return [pltpu.make_async_copy(src, dst, sems.at[slot, g, n]) for n, (src, dst) in enumerate(pieces)]

    def fetch(step, slot):
        for g in range(GROUP):
            for copy in copies(step, slot, g):
                copy.start()

    def dot(a, b):
        return jnp.dot(a, b, preferred_element_type=jnp.float32)

    signed = lax.broadcasted_iota(jnp.int32, (W, 256), 0)
    signed = jnp.where(signed < W // 2, signed, signed - W).astype(jnp.float32)
    win_lane = lax.broadcasted_iota(jnp.int32, (WIN_ROWS, 128), 1)
    base = GROUP * WIN_ROWS

    def turn(x, amount):
        return pltpu.roll(x.astype(jnp.float32), (128 - amount) % 128, axis=1)

    def work(step, slot):
        place_of = []
        for g in range(GROUP):
            h, j = item(step, g)
            _, row_shift, _, col_shift = place(h, j)
            place_of.append((h, j, row_shift))
            parts = [turn(xbuf[slot, g, :, 128 * n : 128 * n + 128], col_shift) for n in range(3)]
            inside = win_lane < 128 - col_shift
            rows = pl.ds(g * WIN_ROWS, WIN_ROWS)
            lines[rows, 0:128] = jnp.where(inside, parts[0], parts[1]).astype(jnp.bfloat16)
            lines[rows, 128:256] = jnp.where(inside, parts[1], parts[2]).astype(jnp.bfloat16)
            rows = pl.ds(base + g * W, W)
            lines[rows, 0:128] = mbuf[slot, g, :, 0:128]
            lines[rows, 128:256] = turn(mbuf[slot, g, :, 128:256], j % 4 * 32).astype(jnp.bfloat16)
        halves[...] = dot(lines[...], cols_tab[...]).astype(jnp.bfloat16)
        spectra = [
            (
                dot(rows_tab[place_of[g][2]], halves[pl.ds(g * WIN_ROWS, WIN_ROWS), :]),
                dot(rows_tab[0, :, 0:W], halves[pl.ds(base + g * W, W), :]),
            )
            for g in range(GROUP)
        ]
        crosses = []
        for g in range(GROUP):
            fixed, moving = spectra[g]
            fcc, fcs, fsc, fss = fixed[:BLK, :128], fixed[:BLK, 128:], fixed[BLK:, :128], fixed[BLK:, 128:]
            mcc, mcs, msc, mss = moving[:BLK, :128], moving[:BLK, 128:], moving[BLK:, :128], moving[BLK:, 128:]
            ee = fcc * mcc + fss * mss + fcs * mcs + fsc * msc
            oo = fcc * mss + fss * mcc - fcs * msc - fsc * mcs
            eo = fcc * mcs - fcs * mcc + fsc * mss - fss * msc
            oe = fcc * msc - fsc * mcc + fcs * mss - fss * mcs
            cross = jnp.concatenate(
                [jnp.concatenate([ee, eo], axis=1), jnp.concatenate([oe, oo], axis=1)], axis=0
            ).astype(jnp.bfloat16)
            crosses.append(cross)
        for g in range(GROUP):
            backs[pl.ds(g * W, W), :] = dot(inv_left[...], crosses[g]).astype(jnp.bfloat16)
        corr = dot(backs[...], inv_right[...])
        for g in range(GROUP):
            h, j, _ = place_of[g]
            energy = corr[g * W : g * W + W]
            energy = energy * energy
            at = pl.ds(h * PATCH_DEV + j % 2 * ROWS + j // 2, 1)
            sum_e[at, :] = jnp.sum(energy, axis=0, keepdims=True)
            sum_r[at, :] = jnp.sum(energy * signed, axis=0, keepdims=True)

    @pl.when(rounds > 0)
    def _():
        fetch(0, 0)

    def one(step, carry):
        slot = step % DEPTH

        @pl.when(step + 1 < rounds)
        def _():
            fetch(step + 1, (step + 1) % DEPTH)

        for g in range(GROUP):
            for copy in copies(step, slot, g):
                copy.wait()
        work(step, slot)
        return carry

    for copy in tables:
        copy.wait()
    lax.fori_loop(0, rounds, one, 0)

    number = lax.broadcasted_iota(jnp.int32, (NY * PATCH_DEV, 256), 1)
    shift = jnp.where(number < W // 2, number, number - W).astype(jnp.float32)
    plain = sum_e[...]
    total = jnp.sum(plain, axis=1, keepdims=True) + EPS
    flows = (
        jnp.sum(sum_r[...], axis=1, keepdims=True) / total,
        jnp.sum(plain * shift, axis=1, keepdims=True) / total,
    )
    lane = lax.broadcasted_iota(jnp.int32, (ROWS, 128), 1)
    for h in range(NY):
        block = jnp.zeros((ROWS, 128), jnp.float32)
        for comp in range(2):
            for side in range(2):
                first = h * PATCH_DEV + side * ROWS
                block = jnp.where(lane == 32 + 64 * side + comp, flows[comp][first : first + ROWS], block)
        out[h] = block


def settle_kernel(
    ep, mob_hbm, own_hbm, flow, out,
    got, total, net, mob_band, u_own, tgt, mob, ua, ub, vel, fsend, frecv, hsend, hrecv, lsem,
):
    t, y, z, c = my_place()
    p = lax.axis_index("pair")
    local = [
        pltpu.make_async_copy(mob_hbm, mob_band, lsem.at[0]),
        pltpu.make_async_copy(own_hbm, u_own, lsem.at[1]),
    ]
    for copy in local:
        copy.start()
    homes = [device_at((y + d) % NY, z, c) for d in range(1, NY)]
    halo = list(halo_targets(t, p))
    greet(homes + [device for _, _, device in halo])
    first = []
    for n, device in enumerate(homes):
        copy = remote(ep.at[(y + n + 1) % NY], got.at[n], fsend.at[n], frecv.at[n], device)
        copy.start()
        first.append(copy)
    span = pl.ds(PAD, SPAN)
    vel[...] = jnp.zeros_like(vel)
    ua[...] = jnp.zeros_like(ua)
    ub[...] = jnp.zeros_like(ub)
    for copy in local:
        copy.wait()
    mob[:, 0, span, :] = mob_band[...]
    for copy in first:
        copy.wait_recv()
    total[...] = ep[y] + got[0] + got[1] + got[2]
    second = []
    for n, (dp, d, device) in enumerate(halo):
        copy = remote(total, net.at[p, pl.ds(ROWS * (2 - d), ROWS), :], hsend.at[n], hrecv.at[n], device)
        copy.start()
        second.append(copy)
    net[p, HALO : HALO + ROWS, :] = total[...]
    for copy in second:
        copy.wait_recv()

    lane = lax.broadcasted_iota(jnp.int32, (SPAN, 128), 1)
    node = (lane == 32) | (lane == 96)
    for s in range(NP):
        values = net[s]
        for comp in range(2):
            turned = values if comp == 0 else pltpu.roll(values, 127, axis=1)
            tgt[s, comp, 0, span, :] = (0.3 / 0.35) * jnp.where(node, turned, 0.0)

    for start in range(0, STEPS, 8):

        @pl.loop(0, 4)
        def _(_):
            for u_in, u_out in ((ua, ub), (ub, ua)):
                relax_step(
                    t, tgt, u_in, u_out, vel, lambda here: mob[:, :, here, :], PAD + start, HIGH - PAD - start, 1
                )

    middle = pl.ds(PAD + HALO, ROWS)
    lane = lax.broadcasted_iota(jnp.int32, (ROWS, 128), 1)
    row = lax.broadcasted_iota(jnp.int32, (ROWS, 128), 0)
    for comp in range(2):
        moved = jnp.zeros((ROWS, 128), jnp.float32)
        given = net[p, HALO : HALO + ROWS, :]
        for s in range(NP):
            moved = jnp.where(p == s, ua[s, comp, 0, middle, :], moved)
        wide, narrow = pltpu.roll(moved, 96, axis=1), pltpu.roll(moved, 32, axis=1)
        for n, (part, inside) in enumerate(((wide, lane >= 96), (wide, lane < 32), (narrow, lane >= 96), (narrow, lane < 32))):
            columns = pl.ds(128 * n, 128)
            out[comp, :, columns] = u_own[comp, :, columns] + jnp.where(inside, part, 0.0)
        even = jnp.sum(jnp.where(lane == 32 + comp, given, 0.0), axis=1, keepdims=True)
        odd = jnp.sum(jnp.where(lane == 96 + comp, given, 0.0), axis=1, keepdims=True)
        spread = jnp.where(lane == 2 * row, even, 0.0) + jnp.where(lane == 2 * row + 1, odd, 0.0)
        flow[comp : comp + 1, :] = jnp.sum(spread, axis=0, keepdims=True)[:, :PATCH_DEV]
    for copy in first + second:
        copy.wait_send()


def make_tables():
    numbers = np.arange(W)
    phase = (numbers[:, None] * numbers[None, :] % W).astype(np.float32) * np.float32(2.0 * math.pi / W)
    scale = np.float32(1.0 / math.sqrt(W))
    cos = (np.cos(phase) * scale).astype(ml_dtypes.bfloat16).astype(np.float32)
    sin = (np.sin(phase) * scale).astype(ml_dtypes.bfloat16).astype(np.float32)
    left = np.zeros((FREQ, W), np.float32)
    left[:HALF], left[BLK : BLK + HALF] = cos[:HALF], sin[:HALF]
    right = np.zeros((W, 256), np.float32)
    right[:, :HALF], right[:, 128 : 128 + HALF] = cos[:, :HALF], sin[:, :HALF]
    rows_tab = np.zeros((17, FREQ, WIN_ROWS), np.float32)
    for shift in range(17):
        rows_tab[shift, :, shift : shift + W] = left
    cols_tab = np.zeros((256, 256), np.float32)
    cols_tab[:W] = right
    weight = np.full((HALF, 1), 2.0, np.float32)
    weight[0] = weight[-1] = 1.0
    inv_left = np.zeros((W, FREQ), np.float32)
    inv_left[:, :HALF], inv_left[:, BLK : BLK + HALF] = (weight * cos[:HALF]).T, (-2.0 * sin[:HALF]).T
    inv_right = np.zeros((256, 256), np.float32)
    inv_right[:HALF, :W], inv_right[128 : 128 + HALF, :W] = weight * cos[:HALF], -2.0 * sin[:HALF]
    half = lambda table: table.astype(ml_dtypes.bfloat16)
    return half(rows_tab), half(cols_tab), half(inv_left), half(inv_right)


def any_spec():
    return pl.BlockSpec(memory_space=pl.ANY)


def hbm_spec():
    return pl.BlockSpec(memory_space=pltpu.HBM)


def vmem_spec():
    return pl.BlockSpec(memory_space=pltpu.VMEM)


def flow_call(gmeta, gi, gpl, gpr):
    f32, bf16 = jnp.float32, jnp.bfloat16
    tables = [jnp.asarray(table) for table in make_tables()]
    return pl.pallas_call(
        flow_kernel,
        out_shape=jax.ShapeDtypeStruct((NY, ROWS, 128), f32),
        in_specs=[pl.BlockSpec(memory_space=pltpu.SMEM)] + [any_spec()] * 3 + [hbm_spec()] * 4,
        out_specs=vmem_spec(),
        scratch_shapes=[
            pltpu.SMEM((NY * PATCH_DEV + 1,), jnp.int32),
            pltpu.VMEM((17, FREQ, WIN_ROWS), bf16),
            pltpu.VMEM((256, 256), bf16),
            pltpu.VMEM((W, FREQ), bf16),
            pltpu.VMEM((256, 256), bf16),
            pltpu.VMEM((DEPTH, GROUP, WIN_ROWS, WIN_COLS), bf16),
            pltpu.VMEM((DEPTH, GROUP, W, 256), bf16),
            pltpu.VMEM((GROUP * (WIN_ROWS + W), 256), bf16),
            pltpu.VMEM((GROUP * (WIN_ROWS + W), 256), bf16),
            pltpu.VMEM((GROUP * W, 256), bf16),
            pltpu.VMEM((NY * PATCH_DEV, 256), f32),
            pltpu.VMEM((NY * PATCH_DEV, 256), f32),
            pltpu.SemaphoreType.DMA((DEPTH, GROUP, 4)),
            pltpu.SemaphoreType.DMA((4,)),
        ],
        compiler_params=pltpu.CompilerParams(vmem_limit_bytes=60 * 2**20),
        name="patch_flows",
    )(gmeta, gi, gpl, gpr, *tables)


def shards(fixed_image, moving_patches, owners, offsets, mobility, prior_flow):
    f32, bf16 = jnp.float32, jnp.bfloat16
    sds = jax.ShapeDtypeStruct
    dma = pltpu.SemaphoreType.DMA
    gi, gpl, gpr, gmeta, u_own, mob_band = pl.pallas_call(
        gather_kernel,
        out_shape=(
            sds((NZ * NC, TILE, TILE), bf16),
            sds((NY, PATCH_DEV, W, 128), bf16),
            sds((NY, PATCH_DEV // 4, W, 128), bf16),
            sds((NY, 8, 128), jnp.int32),
            sds((2, ROWS, COLS), f32),
            sds((NP, SPAN, 128), f32),
        ),
        in_specs=[hbm_spec()] * 6,
        out_specs=(any_spec(), any_spec(), any_spec(), any_spec(), vmem_spec(), vmem_spec()),
        scratch_shapes=[
            pltpu.VMEM((8, 128), jnp.int32),
            pltpu.VMEM((1, PATCH_DEV), jnp.int32),
            pltpu.VMEM((2, PATCH_DEV), jnp.int32),
            pltpu.VMEM((2, ROWS, COLS), f32),
            pltpu.VMEM((ROWS, COLS), f32),
            pltpu.VMEM((PATCH_DEV, W, W), bf16),
            pltpu.VMEM((PATCH_DEV // 4, W, 128), bf16),
            pltpu.VMEM((3, TILES_X, ROWS, 128), f32),
            pltpu.VMEM((NP, 7, ROWS, 128), bf16),
            pltpu.VMEM((NP, 7, SPAN, 128), bf16),
            pltpu.VMEM((NP, 1, 3, HIGH, 128), f32),
            pltpu.VMEM((NP, TILES_X, HIGH, 128), f32),
            pltpu.VMEM((NP, 1, 3, HIGH, 128), f32),
            pltpu.VMEM((NP, 1, 3, HIGH, 128), f32),
            pltpu.VMEM((NP, 1, 3, HIGH, 128), f32),
            pltpu.VMEM((NP, 2, ROWS, 128), f32),
            pltpu.VMEM((NP, 2, ROWS, 128), f32),
            dma((6,)), dma((2, 6)), dma((2, 6)), dma((2, 8)), dma((2, 8)), dma((16,)), dma((16,)),
            dma((3,)), dma((3,)), dma((19,)), dma((19,)), dma((3,)), dma((3,)),
        ],
        compiler_params=pltpu.CompilerParams(
            collective_id=0, has_side_effects=True, vmem_limit_bytes=60 * 2**20
        ),
        name="gather_and_relax",
    )(fixed_image[0], moving_patches[0], owners, offsets[0].T, prior_flow[0], mobility[0])
    ep = flow_call(gmeta, gi, gpl, gpr)
    flow, out = pl.pallas_call(
        settle_kernel,
        out_shape=(sds((2, PATCH_DEV), f32), sds((2, ROWS, COLS), f32)),
        in_specs=[vmem_spec(), any_spec(), any_spec()],
        out_specs=(vmem_spec(), vmem_spec()),
        scratch_shapes=[
            pltpu.VMEM((3, ROWS, 128), f32),
            pltpu.VMEM((ROWS, 128), f32),
            pltpu.VMEM((NP, SPAN, 128), f32),
            pltpu.VMEM((NP, SPAN, 128), f32),
            pltpu.VMEM((2, ROWS, COLS), f32),
            pltpu.VMEM((NP, 2, 1, HIGH, 128), f32),
            pltpu.VMEM((NP, 1, HIGH, 128), f32),
            pltpu.VMEM((NP, 2, 1, HIGH, 128), f32),
            pltpu.VMEM((NP, 2, 1, HIGH, 128), f32),
            pltpu.VMEM((NP, 2, 1, HIGH, 128), f32),
            dma((3,)), dma((3,)), dma((19,)), dma((19,)), dma((2,)),
        ],
        compiler_params=pltpu.CompilerParams(
            collective_id=1, has_side_effects=True, vmem_limit_bytes=32 * 2**20
        ),
        name="share_and_settle",
    )(ep, mob_band, u_own)
    return flow[None], out[None]


def solution(mesh):
    in_specs = (
        P("pair", "tile", None),
        P("pair", "tile", None, None),
        P("pair", "tile"),
        P("pair", "tile", None),
        P("pair", "tile", None),
        P("pair", None, "tile", None),
    )
    out_specs = (P("pair", None, "tile"), P("pair", None, "tile", None))
    return jax.shard_map(shards, mesh=mesh, in_specs=in_specs, out_specs=out_specs, check_vma=False)
```

```python
import functools
import math

import jax
import jax.numpy as jnp
import ml_dtypes
import numpy as np
from jax import lax
from jax.experimental import pallas as pl
from jax.experimental.pallas import tpu as pltpu
from jax.sharding import PartitionSpec as P

MESH = pl.DeviceIdType.MESH
NY, NZ, NC, NP = 4, 8, 2, 4
TILES = NY * NZ * NC
W = 160
TILE = 512
PATCH_DEV = 32
STEPS = 32
EPS = 1e-06
ROWS = 16
COLS = 512
TILES_X = COLS // 128
HALO = 32
PAD = 8
SPAN = ROWS + 2 * HALO
HIGH = SPAN + 2 * PAD
HALF = W // 2 + 1
BLK = 88
FREQ = 2 * BLK
WIN_ROWS = 176
WIN_COLS = 384
GROUP = 8
DEPTH = 2


def device_at(y, z, c):
    return {"tile": (y * NZ + z) * NC + c}


def my_place():
    t = lax.axis_index("tile")
    return t, t // (NZ * NC), (t // NC) % NZ, t % NC


def halo_targets(t, p):
    for dp in range(NP):
        for d in range(-2, 3):
            if dp or d:
                there = {"tile": (t + d + TILES) % TILES, "pair": (p + dp) % NP}
                yield dp, d, there


def remote(src, dst, send, recv, device):
    return pltpu.make_async_remote_copy(
        src_ref=src, dst_ref=dst, send_sem=send, recv_sem=recv, device_id=device, device_id_type=MESH
    )


def greet(devices):
    barrier = pltpu.get_barrier_semaphore()
    for device in devices:
        pl.semaphore_signal(barrier, inc=1, device_id=device, device_id_type=MESH)
    pl.semaphore_wait(barrier, len(devices))


def relax_step(t, target, u_in, u_out, vel, mob, first, last, tiles):
    shape = (NP, tiles, 8, 128)
    lane = lax.broadcasted_iota(jnp.int32, shape, 3)
    line = lax.broadcasted_iota(jnp.int32, shape, 2)
    own = PAD + HALO
    for rows in range(first, last, 8):
        here = pl.ds(rows, 8)
        for comp in range(u_in.shape[1]):
            u = u_in[:, comp, :, here, :]
            above = u_in[:, comp, :, pl.ds(rows - 1, 8), :]
            below = u_in[:, comp, :, pl.ds(rows + 1, 8), :]
            if rows in (own, own - ROWS):
                above = jnp.where((line == 0) & (t == (own - rows) // ROWS), u, above)
            if rows + 8 in (own + ROWS, own + 2 * ROWS):
                below = jnp.where((line == 7) & (t == TILES - (rows + 8 - own) // ROWS), u, below)
            left, right = pltpu.roll(u, 1, axis=3), pltpu.roll(u, 127, axis=3)
            if tiles > 1:
                left = jnp.where(lane == 0, jnp.concatenate([u[:, :1], left[:, :-1]], axis=1), left)
                right = jnp.where(lane == 127, jnp.concatenate([right[:, 1:], u[:, -1:]], axis=1), right)
            inter = jnp.concatenate([u[:1], u[:-1]], axis=0) + jnp.concatenate([u[1:], u[-1:]], axis=0)
            force = ((above + below) + (left + right)) + (0.2 / 0.35) * inter
            force = force + target[:, comp, :, here, :] - (4.0 + 0.7 / 0.35) * u
            speed = 0.8 * vel[:, comp, :, here, :] + mob(here) * force
            vel[:, comp, :, here, :] = speed
            u_out[:, comp, :, here, :] = u + speed


def gather_kernel(
    img, pat, owners, offsets, prior_hbm, mob_hbm, gi, gpl, gpr, gmeta, u_own, mob_band,
    meta, own_v, off_v, prior, mob, pv, pr, fine, own, net, target, mobs, ua, ub, vel, res, got,
    lsem, ysend, yrecv, zsend, zrecv, dsend, drecv, msend, mrecv, hsend, hrecv, rsend, rrecv,
):
    t, y, z, c = my_place()
    p = lax.axis_index("pair")
    right_y, left_y = device_at((y + 1) % NY, z, c), device_at((y + NY - 1) % NY, z, c)
    right_z, left_z = device_at(y, (z + 1) % NZ, c), device_at(y, (z + NZ - 1) % NZ, c)
    across_y = device_at((y + 2) % NY, z, c)
    sibling = device_at(y, z, 1 - c)
    stage = pltpu.make_async_copy(pat, pv, lsem.at[0])
    stage.start()
    strips = [
        pltpu.make_async_copy(prior_hbm, prior, lsem.at[2]),
        pltpu.make_async_copy(mob_hbm, mob, lsem.at[3]),
        pltpu.make_async_copy(owners, own_v, lsem.at[4]),
        pltpu.make_async_copy(offsets, off_v, lsem.at[5]),
    ]
    for copy in strips:
        copy.start()
    mine = z * NC + c
    keep = pltpu.make_async_copy(img, gi.at[mine], lsem.at[1])
    keep.start()
    halo = list(halo_targets(t, p))
    greet([right_y, left_y, across_y, right_z, left_z, sibling] + [device for _, _, device in halo])

    lo, hi = pl.ds(0, 16), pl.ds(16, 16)
    glo, ghi = pl.ds(0, 4), pl.ds(4, 4)
    left_part = pl.ds(0, 128)
    sent = []
    yr, yl = [], []

    def start(copy, into=None):
        copy.start()
        sent.append(copy)
        if into is not None:
            into.append(copy)
        return copy

    def y_left(which, first, side, device, slot):
        return remote(
            pat.at[which, :, left_part], gpl.at[first, which], ysend.at[side, slot], yrecv.at[side, slot], device
        )

    start(y_left(hi, y, 0, right_y, 0), yr)
    start(y_left(lo, y, 1, left_y, 0), yl)

    half = TILE // 2
    zr, zl, dd = [], [], []
    for q in range(2):
        rs = pl.ds(q * half, half)
        start(remote(img.at[rs], gi.at[mine, rs], zsend.at[0, q], zrecv.at[0, q], right_z), zr)
        rs = pl.ds((1 - q) * half, half)
        start(remote(img.at[rs], gi.at[mine, rs], zsend.at[1, q], zrecv.at[1, q], left_z), zl)
    for copy in strips:
        copy.wait()
    meta[0:1, 0:PATCH_DEV] = own_v[...]
    meta[1:3, 0:PATCH_DEV] = off_v[...]
    for n in range(TILES_X):
        columns = pl.ds(128 * n, 128)
        fine[0:2, n] = prior[:, :, columns]
        fine[2, n] = mob[:, columns]
    for v in range(NP):
        own[v, 0:3] = fine[v % 2, v // 2 : v // 2 + 3].astype(jnp.bfloat16)
        own[v, 3:7] = fine[2].astype(jnp.bfloat16)
    e = 1 - 2 * c
    meshes, shared = [], []

    def strip_rows(d):
        return pl.ds(pl.multiple_of(ROWS * (2 + d), ROWS), ROWS)

    def send_strip(dp, d):
        n = len(meshes)
        device = {"tile": (t + d + TILES) % TILES, "pair": (p + dp) % NP}
        copy = remote(own.at[(p + dp) % NP], net.at[p, :, strip_rows(-d), :], hsend.at[n], hrecv.at[n], device)
        start(copy, meshes)

    for dp in range(NP):
        send_strip(dp, -2 * e)
    for dp in range(NP):
        send_strip(dp, 2 * e)
        send_strip(dp, e)
        if dp:
            send_strip(dp, 0)

    def share_strips():
        for dp in range(NP):
            meshes[dp].wait_recv()
            s = (p + NP - dp) % NP
            n = len(meshes) + len(shared)
            copy = remote(
                net.at[s, :, strip_rows(2 * e), :], net.at[s, :, strip_rows(e), :], hsend.at[n], hrecv.at[n], sibling
            )
            start(copy, shared)

    start(y_left(lo, y, 0, right_y, 1), yr)
    start(y_left(hi, y, 1, left_y, 1), yl)
    metas = []
    for n, device in enumerate((right_y, left_y, across_y)):
        start(remote(meta, gmeta.at[y], msend.at[n], mrecv.at[n], device), metas)
    start(remote(img, gi.at[mine], dsend.at[0], drecv.at[0], sibling), dd)

    stage.wait()
    for g in range(PATCH_DEV // 4):
        pr[g] = jnp.concatenate([pv[4 * g + q, :, 128:W] for q in range(4)], axis=1)
    pairs = []
    pairs.append(start(remote(pr.at[ghi], gpr.at[y, ghi], ysend.at[0, 3], yrecv.at[0, 3], right_y)))
    pairs.append(start(remote(pr.at[glo], gpr.at[y, glo], ysend.at[1, 3], yrecv.at[1, 3], left_y)))
    pairs.append(start(remote(pr.at[glo], gpr.at[y, glo], ysend.at[0, 4], yrecv.at[0, 4], right_y)))
    pairs.append(start(remote(pr.at[ghi], gpr.at[y, ghi], ysend.at[1, 4], yrecv.at[1, 4], left_y)))
    local = [
        pltpu.make_async_copy(pv.at[:, :, left_part], gpl.at[y], lsem.at[2]),
        pltpu.make_async_copy(pr, gpr.at[y], lsem.at[3]),
        pltpu.make_async_copy(meta, gmeta.at[y], lsem.at[4]),
    ]
    for copy in local:
        copy.start()

    def forward_z(k, q):
        for side, hops, device in ((0, NZ - k, right_z), (1, k, left_z)):
            slot = ((z + hops) % NZ) * NC + c
            part = q if side == 0 else 1 - q
            rs = pl.ds(part * half, half)
            line = zr if side == 0 else zl
            line[2 * (k - 1) + q].wait_recv()
            block = gi.at[slot, rs]
            if k < 3 or (k == 3 and q == 0):
                start(remote(block, block, zsend.at[side, 2 * k + q], zrecv.at[side, 2 * k + q], device), line)
            n = len(dd)
            start(remote(block, block, dsend.at[n], drecv.at[n], sibling), dd)

    middle = pl.ds(PAD + HALO, ROWS)
    comp, side = p % 2, p // 2

    def begin():
        for copy in meshes[NP:] + shared:
            copy.wait_recv()
        net[p, :, HALO : HALO + ROWS, :] = own[p]
        edge = jnp.zeros((NP, 1, 3, PAD, 128), jnp.float32)
        for ref in (ua, ub):
            ref[:, :, :, 0:PAD, :] = edge
            ref[:, :, :, HIGH - PAD :, :] = edge

        @pl.loop(0, NP)
        def _(s):
            for b in range(SPAN // ROWS):
                rows = pl.ds(PAD + ROWS * b, ROWS)
                values = net[s, :, ROWS * b : ROWS * b + ROWS, :].astype(jnp.float32)
                ua[s, 0, :, rows, :] = values[0:3]
                ub[s, 0, :, rows, :] = values[0:3]
                vel[s, 0, :, rows, :] = jnp.zeros_like(values[0:3])
                target[s, 0, :, rows, :] = (0.3 / 0.35) * values[0:3]
                mobs[s, :, rows, :] = 0.35 * values[3:7]

        values = fine[comp, pl.ds(side, 3)]
        ua[p, 0, :, middle, :] = values
        target[p, 0, :, middle, :] = (0.3 / 0.35) * values
        mobs[p, :, middle, :] = 0.35 * fine[2]

    def relax(first):
        @pl.loop(0, 4)
        def _(_):
            for u_in, u_out in ((ua, ub), (ub, ua)):
                relax_step(
                    t, target, u_in, u_out, vel, lambda here: mobs[:, pl.ds(side, 3), here, :],
                    PAD + first, HIGH - PAD - first, 3,
                )

    def forward_y():
        for copy in (yr[0], yl[0], pairs[0], pairs[1]):
            copy.wait_recv()
        before, after = (y + NY - 1) % NY, (y + 1) % NY
        for side, first, which, groups, device in ((0, before, hi, ghi, right_y), (1, after, lo, glo, left_y)):
            block = gpl.at[first, which]
            start(remote(block, block, ysend.at[side, 2], yrecv.at[side, 2], device), far)
            block = gpr.at[first, groups]
            start(remote(block, block, ysend.at[side, 5], yrecv.at[side, 5], device), far)

    far = []
    forward_z(1, 0)
    forward_z(1, 1)
    share_strips()
    forward_z(2, 0)
    forward_y()
    begin()
    relax(0)
    forward_z(2, 1)
    relax(8)
    forward_z(3, 0)
    relax(16)
    forward_z(3, 1)
    relax(24)
    res[...] = ua[:, 0, pl.ds(side, 2), middle, :]
    results = []
    for d in range(1, NP):
        to = (p + d) % NP
        start(remote(res.at[to], got.at[p], rsend.at[d - 1], rrecv.at[d - 1], {"pair": to}), results)
    got[p] = res[p]
    forward_z(4, 0)
    for copy in results:
        copy.wait_recv()
    for v in range(NP):
        for n in range(2):
            first = 128 * (v // 2 * 2 + n)
            u_own[v % 2, :, first : first + 128] = got[v, n]
    lane = lax.broadcasted_iota(jnp.int32, (SPAN, 128), 1)
    for s in range(NP):
        parts = [mobs[s, n, PAD : PAD + SPAN, :] for n in range(4)]
        low = jnp.where(lane < 32, pltpu.roll(parts[0], 32, axis=1), pltpu.roll(parts[1], 32, axis=1))
        top = jnp.where(lane < 96, pltpu.roll(parts[2], 96, axis=1), pltpu.roll(parts[3], 96, axis=1))
        mob_band[s] = jnp.where(lane < 64, low, top)

    for copy in yr[1:] + yl[1:] + pairs[2:] + far + metas + dd:
        copy.wait_recv()
    for copy in sent:
        copy.wait_send()
    for copy in local:
        copy.wait()
    keep.wait()


def flow_kernel(
    meta, gi, gpl, gpr, rows_hbm, cols_hbm, left_hbm, right_hbm, out,
    items, rows_tab, cols_tab, inv_left, inv_right, xbuf, mbuf, lines, halves, backs, sum_e, sum_r, sems, tsems,
):
    _, y, _, _ = my_place()
    tables = [
        pltpu.make_async_copy(src, dst, tsems.at[n])
        for n, (src, dst) in enumerate(
            ((cols_hbm, cols_tab), (rows_hbm, rows_tab), (left_hbm, inv_left), (right_hbm, inv_right))
        )
    ]

    for copy in tables:
        copy.start()

    def note(h, count):
        for j in range(PATCH_DEV):
            items[count] = h * PATCH_DEV + j
            count = count + (meta[h, 0, j] // (NZ * NC) == y).astype(jnp.int32)
        return count

    count = lax.fori_loop(0, NY, note, jnp.int32(0))
    sum_e[...] = jnp.zeros_like(sum_e)
    sum_r[...] = jnp.zeros_like(sum_r)
    rounds = (count + GROUP - 1) // GROUP

    def item(step, g):
        n = items[jnp.minimum(step * GROUP + g, count - 1)]
        return n // PATCH_DEV, n % PATCH_DEV

    def place(h, j):
        first_row, first_col = meta[h, 1, j], meta[h, 2, j]
        row = jnp.minimum(first_row // 16 * 16, TILE - WIN_ROWS)
        col = first_col // 128 * 128
        return row, first_row - row, col, first_col - col

    def copies(step, slot, g):
        h, j = item(step, g)
        row, _, col, _ = place(h, j)
        image = gi.at[meta[h, 0, j] % (NZ * NC)]
        rows = pl.ds(pl.multiple_of(row, 16), WIN_ROWS)
        third = jnp.minimum(col + 256, TILE - 128)
        pieces = (
            (image.at[rows, pl.ds(pl.multiple_of(col, 128), 256)], xbuf.at[slot, g, :, pl.ds(0, 256)]),
            (image.at[rows, pl.ds(pl.multiple_of(third, 128), 128)], xbuf.at[slot, g, :, pl.ds(256, 128)]),
            (gpl.at[h, j], mbuf.at[slot, g, :, pl.ds(0, 128)]),
            (gpr.at[h, j // 4], mbuf.at[slot, g, :, pl.ds(128, 128)]),
        )
        return [pltpu.make_async_copy(src, dst, sems.at[slot, g, n]) for n, (src, dst) in enumerate(pieces)]

    def fetch(step, slot):
        for g in range(GROUP):
            for copy in copies(step, slot, g):
                copy.start()

    def dot(a, b):
        return jnp.dot(a, b, preferred_element_type=jnp.float32)

    signed = lax.broadcasted_iota(jnp.int32, (W, 256), 0)
    signed = jnp.where(signed < W // 2, signed, signed - W).astype(jnp.float32)
    win_lane = lax.broadcasted_iota(jnp.int32, (WIN_ROWS, 128), 1)
    base = GROUP * WIN_ROWS

    def turn(x, amount):
        return pltpu.roll(x.astype(jnp.float32), (128 - amount) % 128, axis=1)

    def work(step, slot):
        place_of = []
        for g in range(GROUP):
            h, j = item(step, g)
            _, row_shift, _, col_shift = place(h, j)
            place_of.append((h, j, row_shift))
            parts = [turn(xbuf[slot, g, :, 128 * n : 128 * n + 128], col_shift) for n in range(3)]
            inside = win_lane < 128 - col_shift
            rows = pl.ds(g * WIN_ROWS, WIN_ROWS)
            lines[rows, 0:128] = jnp.where(inside, parts[0], parts[1]).astype(jnp.bfloat16)
            lines[rows, 128:256] = jnp.where(inside, parts[1], parts[2]).astype(jnp.bfloat16)
            rows = pl.ds(base + g * W, W)
            lines[rows, 0:128] = mbuf[slot, g, :, 0:128]
            lines[rows, 128:256] = turn(mbuf[slot, g, :, 128:256], j % 4 * 32).astype(jnp.bfloat16)
        halves[...] = dot(lines[...], cols_tab[...]).astype(jnp.bfloat16)
        spectra = [
            (
                dot(rows_tab[place_of[g][2]], halves[pl.ds(g * WIN_ROWS, WIN_ROWS), :]),
                dot(rows_tab[0, :, 0:W], halves[pl.ds(base + g * W, W), :]),
            )
            for g in range(GROUP)
        ]
        crosses = []
        for g in range(GROUP):
            fixed, moving = spectra[g]
            fcc, fcs, fsc, fss = fixed[:BLK, :128], fixed[:BLK, 128:], fixed[BLK:, :128], fixed[BLK:, 128:]
            mcc, mcs, msc, mss = moving[:BLK, :128], moving[:BLK, 128:], moving[BLK:, :128], moving[BLK:, 128:]
            ee = fcc * mcc + fss * mss + fcs * mcs + fsc * msc
            oo = fcc * mss + fss * mcc - fcs * msc - fsc * mcs
            eo = fcc * mcs - fcs * mcc + fsc * mss - fss * msc
            oe = fcc * msc - fsc * mcc + fcs * mss - fss * mcs
            cross = jnp.concatenate(
                [jnp.concatenate([ee, eo], axis=1), jnp.concatenate([oe, oo], axis=1)], axis=0
            ).astype(jnp.bfloat16)
            crosses.append(cross)
        for g in range(GROUP):
            backs[pl.ds(g * W, W), :] = dot(inv_left[...], crosses[g]).astype(jnp.bfloat16)
        corr = dot(backs[...], inv_right[...])
        for g in range(GROUP):
            h, j, _ = place_of[g]
            energy = corr[g * W : g * W + W]
            energy = energy * energy
            at = pl.ds(h * PATCH_DEV + j % 2 * ROWS + j // 2, 1)
            sum_e[at, :] = jnp.sum(energy, axis=0, keepdims=True)
            sum_r[at, :] = jnp.sum(energy * signed, axis=0, keepdims=True)

    @pl.when(rounds > 0)
    def _():
        fetch(0, 0)

    def one(step, carry):
        slot = step % DEPTH

        @pl.when(step + 1 < rounds)
        def _():
            fetch(step + 1, (step + 1) % DEPTH)

        for g in range(GROUP):
            for copy in copies(step, slot, g):
                copy.wait()
        work(step, slot)
        return carry

    for copy in tables:
        copy.wait()
    lax.fori_loop(0, rounds, one, 0)

    number = lax.broadcasted_iota(jnp.int32, (NY * PATCH_DEV, 256), 1)
    shift = jnp.where(number < W // 2, number, number - W).astype(jnp.float32)
    plain = sum_e[...]
    total = jnp.sum(plain, axis=1, keepdims=True) + EPS
    flows = (
        jnp.sum(sum_r[...], axis=1, keepdims=True) / total,
        jnp.sum(plain * shift, axis=1, keepdims=True) / total,
    )
    lane = lax.broadcasted_iota(jnp.int32, (ROWS, 128), 1)
    for h in range(NY):
        block = jnp.zeros((ROWS, 128), jnp.float32)
        for comp in range(2):
            for side in range(2):
                first = h * PATCH_DEV + side * ROWS
                block = jnp.where(lane == 32 + 64 * side + comp, flows[comp][first : first + ROWS], block)
        out[h] = block


def settle_kernel(
    ep, mob_hbm, own_hbm, flow, out,
    got, total, net, mob_band, u_own, tgt, mob, ua, ub, vel, fsend, frecv, hsend, hrecv, lsem,
):
    t, y, z, c = my_place()
    p = lax.axis_index("pair")
    local = [
        pltpu.make_async_copy(mob_hbm, mob_band, lsem.at[0]),
        pltpu.make_async_copy(own_hbm, u_own, lsem.at[1]),
    ]
    for copy in local:
        copy.start()
    homes = [device_at((y + d) % NY, z, c) for d in range(1, NY)]
    halo = list(halo_targets(t, p))
    greet(homes + [device for _, _, device in halo])
    first = []
    for n, device in enumerate(homes):
        copy = remote(ep.at[(y + n + 1) % NY], got.at[n], fsend.at[n], frecv.at[n], device)
        copy.start()
        first.append(copy)
    span = pl.ds(PAD, SPAN)
    vel[...] = jnp.zeros_like(vel)
    ua[...] = jnp.zeros_like(ua)
    ub[...] = jnp.zeros_like(ub)
    for copy in local:
        copy.wait()
    mob[:, 0, span, :] = mob_band[...]
    for copy in first:
        copy.wait_recv()
    total[...] = ep[y] + got[0] + got[1] + got[2]
    second = []
    for n, (dp, d, device) in enumerate(halo):
        copy = remote(total, net.at[p, pl.ds(ROWS * (2 - d), ROWS), :], hsend.at[n], hrecv.at[n], device)
        copy.start()
        second.append(copy)
    net[p, HALO : HALO + ROWS, :] = total[...]
    for copy in second:
        copy.wait_recv()

    lane = lax.broadcasted_iota(jnp.int32, (SPAN, 128), 1)
    node = (lane == 32) | (lane == 96)
    for s in range(NP):
        values = net[s]
        for comp in range(2):
            turned = values if comp == 0 else pltpu.roll(values, 127, axis=1)
            tgt[s, comp, 0, span, :] = (0.3 / 0.35) * jnp.where(node, turned, 0.0)

    for start in range(0, STEPS, 8):

        @pl.loop(0, 4)
        def _(_):
            for u_in, u_out in ((ua, ub), (ub, ua)):
                relax_step(
                    t, tgt, u_in, u_out, vel, lambda here: mob[:, :, here, :], PAD + start, HIGH - PAD - start, 1
                )

    middle = pl.ds(PAD + HALO, ROWS)
    lane = lax.broadcasted_iota(jnp.int32, (ROWS, 128), 1)
    row = lax.broadcasted_iota(jnp.int32, (ROWS, 128), 0)
    for comp in range(2):
        moved = jnp.zeros((ROWS, 128), jnp.float32)
        given = net[p, HALO : HALO + ROWS, :]
        for s in range(NP):
            moved = jnp.where(p == s, ua[s, comp, 0, middle, :], moved)
        wide, narrow = pltpu.roll(moved, 96, axis=1), pltpu.roll(moved, 32, axis=1)
        for n, (part, inside) in enumerate(((wide, lane >= 96), (wide, lane < 32), (narrow, lane >= 96), (narrow, lane < 32))):
            columns = pl.ds(128 * n, 128)
            out[comp, :, columns] = u_own[comp, :, columns] + jnp.where(inside, part, 0.0)
        even = jnp.sum(jnp.where(lane == 32 + comp, given, 0.0), axis=1, keepdims=True)
        odd = jnp.sum(jnp.where(lane == 96 + comp, given, 0.0), axis=1, keepdims=True)
        spread = jnp.where(lane == 2 * row, even, 0.0) + jnp.where(lane == 2 * row + 1, odd, 0.0)
        flow[comp : comp + 1, :] = jnp.sum(spread, axis=0, keepdims=True)[:, :PATCH_DEV]
    for copy in first + second:
        copy.wait_send()


def make_tables():
    numbers = np.arange(W)
    phase = (numbers[:, None] * numbers[None, :] % W).astype(np.float32) * np.float32(2.0 * math.pi / W)
    scale = np.float32(1.0 / math.sqrt(W))
    cos = (np.cos(phase) * scale).astype(ml_dtypes.bfloat16).astype(np.float32)
    sin = (np.sin(phase) * scale).astype(ml_dtypes.bfloat16).astype(np.float32)
    left = np.zeros((FREQ, W), np.float32)
    left[:HALF], left[BLK : BLK + HALF] = cos[:HALF], sin[:HALF]
    right = np.zeros((W, 256), np.float32)
    right[:, :HALF], right[:, 128 : 128 + HALF] = cos[:, :HALF], sin[:, :HALF]
    rows_tab = np.zeros((17, FREQ, WIN_ROWS), np.float32)
    for shift in range(17):
        rows_tab[shift, :, shift : shift + W] = left
    cols_tab = np.zeros((256, 256), np.float32)
    cols_tab[:W] = right
    weight = np.full((HALF, 1), 2.0, np.float32)
    weight[0] = weight[-1] = 1.0
    inv_left = np.zeros((W, FREQ), np.float32)
    inv_left[:, :HALF], inv_left[:, BLK : BLK + HALF] = (weight * cos[:HALF]).T, (-2.0 * sin[:HALF]).T
    inv_right = np.zeros((256, 256), np.float32)
    inv_right[:HALF, :W], inv_right[128 : 128 + HALF, :W] = weight * cos[:HALF], -2.0 * sin[:HALF]
    half = lambda table: table.astype(ml_dtypes.bfloat16)
    return half(rows_tab), half(cols_tab), half(inv_left), half(inv_right)


def any_spec():
    return pl.BlockSpec(memory_space=pl.ANY)


def hbm_spec():
    return pl.BlockSpec(memory_space=pltpu.HBM)


def vmem_spec():
    return pl.BlockSpec(memory_space=pltpu.VMEM)


def flow_call(gmeta, gi, gpl, gpr):
    f32, bf16 = jnp.float32, jnp.bfloat16
    tables = [jnp.asarray(table) for table in make_tables()]
    return pl.pallas_call(
        flow_kernel,
        out_shape=jax.ShapeDtypeStruct((NY, ROWS, 128), f32),
        in_specs=[pl.BlockSpec(memory_space=pltpu.SMEM)] + [any_spec()] * 3 + [hbm_spec()] * 4,
        out_specs=vmem_spec(),
        scratch_shapes=[
            pltpu.SMEM((NY * PATCH_DEV + 1,), jnp.int32),
            pltpu.VMEM((17, FREQ, WIN_ROWS), bf16),
            pltpu.VMEM((256, 256), bf16),
            pltpu.VMEM((W, FREQ), bf16),
            pltpu.VMEM((256, 256), bf16),
            pltpu.VMEM((DEPTH, GROUP, WIN_ROWS, WIN_COLS), bf16),
            pltpu.VMEM((DEPTH, GROUP, W, 256), bf16),
            pltpu.VMEM((GROUP * (WIN_ROWS + W), 256), bf16),
            pltpu.VMEM((GROUP * (WIN_ROWS + W), 256), bf16),
            pltpu.VMEM((GROUP * W, 256), bf16),
            pltpu.VMEM((NY * PATCH_DEV, 256), f32),
            pltpu.VMEM((NY * PATCH_DEV, 256), f32),
            pltpu.SemaphoreType.DMA((DEPTH, GROUP, 4)),
            pltpu.SemaphoreType.DMA((4,)),
        ],
        compiler_params=pltpu.CompilerParams(vmem_limit_bytes=60 * 2**20),
        name="patch_flows",
    )(gmeta, gi, gpl, gpr, *tables)


def shards(fixed_image, moving_patches, owners, offsets, mobility, prior_flow):
    f32, bf16 = jnp.float32, jnp.bfloat16
    sds = jax.ShapeDtypeStruct
    dma = pltpu.SemaphoreType.DMA
    gi, gpl, gpr, gmeta, u_own, mob_band = pl.pallas_call(
        gather_kernel,
        out_shape=(
            sds((NZ * NC, TILE, TILE), bf16),
            sds((NY, PATCH_DEV, W, 128), bf16),
            sds((NY, PATCH_DEV // 4, W, 128), bf16),
            sds((NY, 8, 128), jnp.int32),
            sds((2, ROWS, COLS), f32),
            sds((NP, SPAN, 128), f32),
        ),
        in_specs=[hbm_spec()] * 6,
        out_specs=(any_spec(), any_spec(), any_spec(), any_spec(), vmem_spec(), vmem_spec()),
        scratch_shapes=[
            pltpu.VMEM((8, 128), jnp.int32),
            pltpu.VMEM((1, PATCH_DEV), jnp.int32),
            pltpu.VMEM((2, PATCH_DEV), jnp.int32),
            pltpu.VMEM((2, ROWS, COLS), f32),
            pltpu.VMEM((ROWS, COLS), f32),
            pltpu.VMEM((PATCH_DEV, W, W), bf16),
            pltpu.VMEM((PATCH_DEV // 4, W, 128), bf16),
            pltpu.VMEM((3, TILES_X, ROWS, 128), f32),
            pltpu.VMEM((NP, 7, ROWS, 128), bf16),
            pltpu.VMEM((NP, 7, SPAN, 128), bf16),
            pltpu.VMEM((NP, 1, 3, HIGH, 128), f32),
            pltpu.VMEM((NP, TILES_X, HIGH, 128), f32),
            pltpu.VMEM((NP, 1, 3, HIGH, 128), f32),
            pltpu.VMEM((NP, 1, 3, HIGH, 128), f32),
            pltpu.VMEM((NP, 1, 3, HIGH, 128), f32),
            pltpu.VMEM((NP, 2, ROWS, 128), f32),
            pltpu.VMEM((NP, 2, ROWS, 128), f32),
            dma((6,)), dma((2, 6)), dma((2, 6)), dma((2, 8)), dma((2, 8)), dma((16,)), dma((16,)),
            dma((3,)), dma((3,)), dma((19,)), dma((19,)), dma((3,)), dma((3,)),
        ],
        compiler_params=pltpu.CompilerParams(
            collective_id=0, has_side_effects=True, vmem_limit_bytes=60 * 2**20
        ),
        name="gather_and_relax",
    )(fixed_image[0], moving_patches[0], owners, offsets[0].T, prior_flow[0], mobility[0])
    ep = flow_call(gmeta, gi, gpl, gpr)
    flow, out = pl.pallas_call(
        settle_kernel,
        out_shape=(sds((2, PATCH_DEV), f32), sds((2, ROWS, COLS), f32)),
        in_specs=[vmem_spec(), any_spec(), any_spec()],
        out_specs=(vmem_spec(), vmem_spec()),
        scratch_shapes=[
            pltpu.VMEM((3, ROWS, 128), f32),
            pltpu.VMEM((ROWS, 128), f32),
            pltpu.VMEM((NP, SPAN, 128), f32),
            pltpu.VMEM((NP, SPAN, 128), f32),
            pltpu.VMEM((2, ROWS, COLS), f32),
            pltpu.VMEM((NP, 2, 1, HIGH, 128), f32),
            pltpu.VMEM((NP, 1, HIGH, 128), f32),
            pltpu.VMEM((NP, 2, 1, HIGH, 128), f32),
            pltpu.VMEM((NP, 2, 1, HIGH, 128), f32),
            pltpu.VMEM((NP, 2, 1, HIGH, 128), f32),
            dma((3,)), dma((3,)), dma((19,)), dma((19,)), dma((2,)),
        ],
        compiler_params=pltpu.CompilerParams(
            collective_id=1, has_side_effects=True, vmem_limit_bytes=32 * 2**20
        ),
        name="share_and_settle",
    )(ep, mob_band, u_own)
    return flow[None], out[None]


def solution(mesh):
    in_specs = (
        P("pair", "tile", None),
        P("pair", "tile", None, None),
        P("pair", "tile"),
        P("pair", "tile", None),
        P("pair", "tile", None),
        P("pair", None, "tile", None),
    )
    out_specs = (P("pair", None, "tile"), P("pair", None, "tile", None))
    return jax.shard_map(shards, mesh=mesh, in_specs=in_specs, out_specs=out_specs, check_vma=False)
```
